768 devices in a mesh: tx: 96 (over y, z), ty: 8 (over x, core).
Axes of the slice: x: 4, y: 8, z: 12, core: 2. Of those that a mesh axis runs over, the one named last changes fastest.
Arguments:
- state: bfloat16 [786432, 128], P(('tx', 'ty')), may hold values from -6 to 6
- departures: bfloat16 [147456, 256], P(('tx', 'ty')), may hold values from -6 to 6
- stencil: int32 [147456, 4], P(('tx', 'ty')), may hold values from 0 to 1023, as said below
- bilinear: bfloat16 [147456, 4], P(('tx', 'ty')), may hold values from 0 to 1, as said below
- counts: int32 [73728], P(('tx', 'ty')), may hold values from 0 to 2, as said below
- predictors: float32 [8, 147456], P(None, ('tx', 'ty')), may hold values from -6 to 6
- w_in: bfloat16 [128, 512], replicated, may hold values from -0.5 to 0.5
- b_in: float32 [512], replicated, may hold values from -3 to 3
- w_mid: bfloat16 [512, 512], replicated, may hold values from -0.25 to 0.25
- b_mid: float32 [512], replicated, may hold values from -3 to 3
- w_out: bfloat16 [512, 256], replicated, may hold values from -0.25 to 0.25
- b_out: float32 [256], replicated, may hold values from -4 to 4
Outputs:
- radiance: bfloat16 [147456, 256], P(('tx', 'ty'))
- state_grad: float32 [786432, 128], P(('tx', 'ty'))
- bias_grad: float32 [8, 256], replicated
The draws below stay inside these ranges and needn't reach their ends.
Inputs may be any that keep to these rules, and one draw needn't show every extreme that they name: `stencil`: the four entries are c, c + 1, c + 32, c + 33 for a corner c of the owner's 32 x 32 tile. Nonnegative bilinear weights of two fractions; the four sum to one up to rounding. Only the first counts slots of each block of 2 are live. In every draw one tx index receives 2 live slots from every holder.
All inputs are finite; a program needn't handle non-finite values.
Results may differ from the reference program's by a relative error of at most 0.0075.
Values may be sent and summed in bfloat16 or wider, within the bound.
No kernel may reach another device: no remote copies, remote signals or barrier semaphores. Data moves between devices by JAX's collectives and lax.ppermute only.
A program may use at most 32 MiB of HBM per device.

```python
import math
import jax
import jax.numpy as jnp
from jax import lax

FEAT = 128
HID = 512
CH = 256
NPRED = 8
TILE_W = 32
CAP = 2
COL_DEV = 1024
SLOTS = 192
OBS_ALL = 147456
COLS = 786432
N_TX = 96
N_TY = 8
DEVICES = 768


def draw_stencil(key, part):
    key = jax.random.fold_in(key, 23)
    key_row, key_col = jax.random.split(key)
    row = jax.random.randint(key_row, (OBS_ALL,), 0, TILE_W - 1)
    column = jax.random.randint(key_col, (OBS_ALL,), 0, TILE_W - 1)
    corner = row * TILE_W + column
    corner = corner.at[0].set(0).at[1].set((TILE_W - 2) * TILE_W + TILE_W - 2)
    return jnp.stack([corner, corner + 1, corner + TILE_W, corner + TILE_W + 1], axis=1).astype(jnp.int32)


def draw_bilinear(key, part):
    key = jax.random.fold_in(key, 37)
    key_x, key_y = jax.random.split(key)
    frac_x = jax.random.uniform(key_x, (OBS_ALL,), jnp.float32)
    frac_y = jax.random.uniform(key_y, (OBS_ALL,), jnp.float32)
    weights = jnp.stack([(1.0 - frac_x) * (1.0 - frac_y), frac_x * (1.0 - frac_y), (1.0 - frac_x) * frac_y, frac_x * frac_y], axis=1)
    return weights.astype(jnp.bfloat16)


def draw_counts(key, part):
    key = jax.random.fold_in(key, 51)
    key_base, key_full = jax.random.split(key)
    base = jax.random.randint(key_base, (DEVICES, N_TX), 0, CAP + 1)
    target = jax.random.randint(key_full, (), 0, N_TX)
    base = jnp.where(jnp.arange(N_TX)[None, :] == target, CAP, base)
    return base.reshape(-1).astype(jnp.int32)


def levels(own_key, shape, pieces, low, high):
    level, own = 1.0, jax.random.fold_in(own_key, 6)
    for dim, blocks in pieces:
        draws = jnp.exp(jax.random.uniform(jax.random.fold_in(own, dim), (blocks,), jnp.float32, low / len(pieces), high / len(pieces)))
        level = level * jnp.repeat(draws, shape[dim] // blocks).reshape([-1 if axis == dim else 1 for axis in range(len(shape))])
    return level


def bell_draw(stream_key, extent, spread, reach, cuts=(), held_as=jnp.bfloat16):
    entries = jax.random.normal(stream_key, extent, jnp.float32) * spread
    if len(cuts) > 0:
        entries = levels(stream_key, extent, cuts, -0.22, 0.18) * entries
    return jnp.clip(entries, min=-reach, max=reach).astype(held_as)


def setup_inputs(seed: int = 0) -> dict:
    key_of = jax.random.split(jax.random.key(seed), 13)
    state = bell_draw(key_of[0], (COLS, FEAT), 1.0, 6.0, ((0, 768),))
    departures = bell_draw(key_of[1], (OBS_ALL, CH), 1.0, 6.0, ((0, 768),))
    stencil = draw_stencil(jax.random.fold_in(key_of[12], 71), 0)
    bilinear = draw_bilinear(jax.random.fold_in(key_of[12], 71), 0)
    counts = draw_counts(jax.random.fold_in(key_of[12], 71), 0)
    predictors = bell_draw(key_of[5], (NPRED, OBS_ALL), 1.0, 6.0, ((1, 768),), jnp.float32)
    w_in = bell_draw(key_of[6], (FEAT, HID), FEAT ** -0.5, 0.5)
    b_in = bell_draw(key_of[7], (HID,), 0.5, 3.0, (), jnp.float32)
    w_mid = bell_draw(key_of[8], (HID, HID), HID ** -0.5, 0.25)
    b_mid = bell_draw(key_of[9], (HID,), 0.5, 3.0, (), jnp.float32)
    w_out = bell_draw(key_of[10], (HID, CH), HID ** -0.5, 0.25)
    b_out = bell_draw(key_of[11], (CH,), 1.0, 4.0, (), jnp.float32)
    return dict(state=state, departures=departures, stencil=stencil, bilinear=bilinear, counts=counts, predictors=predictors, w_in=w_in, b_in=b_in, w_mid=w_mid, b_mid=b_mid, w_out=w_out, b_out=b_out)


def reference(state, departures, stencil, bilinear, counts, predictors, w_in, b_in, w_mid, b_mid, w_out, b_out):
    holder = jnp.arange(DEVICES, dtype=jnp.int32)
    slot = jnp.arange(SLOTS, dtype=jnp.int32)
    owner = slot[None, :] // CAP * N_TY + holder[:, None] % N_TY
    cols = owner.reshape(-1)[:, None] * COL_DEV + stencil
    count_of = counts.reshape(DEVICES, N_TX)[:, slot // CAP]
    live = (slot[None, :] % CAP < count_of).reshape(-1)
    dy = jnp.where(live[:, None], departures, jnp.zeros_like(departures))
    profile = jnp.zeros((OBS_ALL, FEAT), jnp.float32)
    for k in range(4):
        profile = profile + bilinear[:, k:k + 1].astype(jnp.float32) * state[cols[:, k]].astype(jnp.float32)
    profile = profile.astype(jnp.bfloat16)
    h1 = jnp.tanh(jnp.dot(profile, w_in, preferred_element_type=jnp.float32) + b_in).astype(jnp.bfloat16)
    h2 = jnp.tanh(jnp.dot(h1, w_mid, preferred_element_type=jnp.float32) + b_mid).astype(jnp.bfloat16)
    radiance = (jnp.dot(h2, w_out, preferred_element_type=jnp.float32) + b_out).astype(jnp.bfloat16)
    h2f = h2.astype(jnp.float32)
    h1f = h1.astype(jnp.float32)
    g2 = (jnp.dot(dy, w_out.T, preferred_element_type=jnp.float32) * (1.0 - h2f * h2f)).astype(jnp.bfloat16)
    g1 = (jnp.dot(g2, w_mid.T, preferred_element_type=jnp.float32) * (1.0 - h1f * h1f)).astype(jnp.bfloat16)
    dprofile = jnp.dot(g1, w_in.T, preferred_element_type=jnp.float32).astype(jnp.bfloat16)
    state_grad = jnp.zeros((COLS, FEAT), jnp.float32)
    for k in range(4):
        state_grad = state_grad.at[cols[:, k]].add(bilinear[:, k:k + 1].astype(jnp.float32) * dprofile.astype(jnp.float32))
    bias_grad = jnp.dot(predictors, dy.astype(jnp.float32), precision=lax.Precision.HIGHEST) * (1.0 / math.sqrt(OBS_ALL))
    return (radiance, state_grad, bias_grad)
```

```python
import math

import jax
import jax.numpy as jnp
from jax import lax
from jax.sharding import PartitionSpec as P

F32, BF16 = jnp.float32, jnp.bfloat16


def exchange(block, axis):
    return lax.all_to_all(block, axis, split_axis=0, concat_axis=0, tiled=True)


def split_pair(x):
    high = lax.reduce_precision(x, exponent_bits=8, mantissa_bits=7)
    return high.astype(BF16), (x - high).astype(BF16)


def forward(profile, w_in, b_in, w_mid, b_mid):
    h1 = jnp.tanh(jnp.dot(profile, w_in, preferred_element_type=F32) + b_in).astype(BF16)
    h2 = jnp.tanh(jnp.dot(h1, w_mid, preferred_element_type=F32) + b_mid).astype(BF16)
    return h1, h2


def backward(cotangent, h1, h2, w_in, w_mid, w_out):
    back_dims = (((1,), (1,)), ((), ()))
    h2f, h1f = h2.astype(F32), h1.astype(F32)
    g2 = lax.dot_general(cotangent, w_out, back_dims, preferred_element_type=F32)
    g2 = (g2 * (1.0 - h2f * h2f)).astype(BF16)
    g1 = lax.dot_general(g2, w_mid, back_dims, preferred_element_type=F32)
    g1 = (g1 * (1.0 - h1f * h1f)).astype(BF16)
    return lax.dot_general(g1, w_in, back_dims, preferred_element_type=F32).astype(BF16)


def on_device(
    state, departures, stencil, bilinear, counts, predictors, w_in, b_in, w_mid, b_mid, w_out, b_out
):
    slots, channels = departures.shape
    columns, feat = state.shape
    npred = predictors.shape[0]
    peers = lax.axis_size("tx")
    rows = lax.axis_size("ty")
    cap = slots // peers
    tile_w = 32
    total_slots = slots * peers * rows
    share = -(-npred * channels // slots)

    live = (jnp.arange(cap, dtype=jnp.int32)[None, :] < counts[:, None]).reshape(slots)
    dy = jnp.where(live[:, None], departures, jnp.zeros_like(departures))
    partial = jnp.dot(predictors, dy.astype(F32), precision=lax.Precision.HIGHEST)
    partial = jnp.pad(partial.reshape(-1), (0, share * slots - npred * channels)).reshape(slots, share)
    high, low = split_pair(partial)
    corner = stencil[:, 0]
    place = jnp.stack([corner // tile_w, corner % tile_w], axis=1).astype(BF16)
    used = 6 + 2 * share
    pad = jnp.zeros((slots, 128 - used), BF16)
    sent = jnp.concatenate([dy, place, bilinear, high, low, pad], axis=1)
    got = exchange(sent.reshape(peers, cap, -1), "tx").reshape(slots, -1)

    got_dy = got[:, :channels]
    extra = got[:, channels:].astype(F32)
    terms = extra[:, 6 : 6 + share] + extra[:, 6 + share : 6 + 2 * share]
    terms = terms.reshape(peers, cap * share).sum(axis=0)
    spread_terms = jnp.broadcast_to(jnp.pad(terms, (0, 128 - cap * share))[None, None], (rows, 1, 128))
    terms = exchange(spread_terms, "ty").sum(axis=(0, 1))[: cap * share]
    terms = terms * (1.0 / math.sqrt(total_slots))
    high, low = split_pair(terms.reshape(cap, share))

    first = (extra[:, 0:1] * tile_w + extra[:, 1:2]).astype(jnp.int32)
    delta = jnp.arange(columns, dtype=jnp.int32)[None, :] - first
    spread = jnp.zeros((slots, columns), F32)
    for k, offset in enumerate((0, 1, tile_w, tile_w + 1)):
        spread = jnp.where(delta == offset, extra[:, 2 + k : 3 + k], spread)
    spread = spread.astype(BF16)
    profile = jnp.dot(spread, state, preferred_element_type=F32).astype(BF16)

    tail = jnp.concatenate([high, low, jnp.zeros((cap, 128 - 2 * share), BF16)], axis=1)
    tail = jnp.broadcast_to(tail[None], (peers, cap, 128))
    back = exchange(jnp.concatenate([profile.reshape(peers, cap, feat), tail], axis=2), "tx")

    h1, h2 = forward(profile, w_in, b_in, w_mid, b_mid)
    dprofile = backward(got_dy, h1, h2, w_in, w_mid, w_out)
    state_grad = lax.dot_general(
        spread, dprofile, (((0,), (0,)), ((), ())), preferred_element_type=F32
    )

    back = back.reshape(slots, -1)
    mine = back[:, :feat]
    bias = back[:, feat : feat + 2 * share].astype(F32)
    bias_grad = (bias[:, :share] + bias[:, share:]).reshape(-1)[: npred * channels]
    bias_grad = bias_grad.reshape(npred, channels)
    h1, h2 = forward(mine, w_in, b_in, w_mid, b_mid)
    radiance = (jnp.dot(h2, w_out, preferred_element_type=F32) + b_out).astype(BF16)
    return (radiance, state_grad, bias_grad)


def solution(mesh):
    both = P(("tx", "ty"), None)
    placed = (both, both, both, both, P(("tx", "ty")), P(None, ("tx", "ty"))) + (P(),) * 6
    return jax.shard_map(
        on_device,
        mesh=mesh,
        in_specs=placed,
        out_specs=(both, both, P()),
        check_vma=False,
    )
```

```python
import functools
import math

import jax
import jax.numpy as jnp
from jax import lax
from jax.experimental import pallas as pl
from jax.experimental.pallas import tpu as pltpu
from jax.sharding import PartitionSpec as P

F32, BF16, I32 = jnp.float32, jnp.bfloat16, jnp.int32
NT = (((1,), (1,)), ((), ()))
TN = (((0,), (0,)), ((), ()))
TILE_W = 32
LANES = 128
GRANT = 40 * 1024 * 1024


def exchange(block, axis):
    return lax.all_to_all(block, axis, split_axis=0, concat_axis=0, tiled=True)


def dot(a, b):
    return jnp.dot(a, b, preferred_element_type=F32)


def dot_dims(a, b, dims):
    return lax.dot_general(a, b, dims, preferred_element_type=F32)


def place(shape, dim):
    return lax.broadcasted_iota(I32, shape, dim)


def identity(rows, columns):
    shape = (rows, columns)
    return (place(shape, 0) == place(shape, 1)).astype(F32).astype(BF16)


def rounded(x):
    return x.astype(BF16).astype(F32)


def pack_kernel(departures, stencil, bilinear, counts, predictors, out):
    slots, channels = departures.shape
    peers = counts.shape[1]
    cap = slots // peers
    npred = predictors.shape[0]
    holds = (place((slots, peers), 0) // cap == place((slots, peers), 1)).astype(F32).astype(BF16)
    counted = jnp.broadcast_to(counts[...].astype(F32), (8, peers)).astype(BF16)
    count_of = dot_dims(holds, counted, NT)[:, 0:1]
    live = (place((slots, 1), 0) % cap).astype(F32) < count_of
    dy = jnp.where(live, departures[...].astype(F32), 0.0).astype(BF16)
    out[:, :channels] = dy

    pred = predictors[...]
    part0 = rounded(pred)
    part1 = rounded(pred - part0)
    part2 = pred - part0 - part1
    thirds = dot(jnp.concatenate([part0, part1, part2], axis=0).astype(BF16), dy)
    partial = thirds[:npred] + thirds[npred : 2 * npred] + thirds[2 * npred :]
    rest = channels - LANES
    upper = jnp.where(
        place((npred, rest), 1) >= slots - LANES, partial[:, LANES:], 0.0
    )
    upper = jnp.concatenate([upper, jnp.zeros((npred, slots - rest), F32)], axis=1)
    lower = partial[:, :slots]
    corner = stencil[0:1, :]
    column = jnp.bitwise_and(corner, TILE_W - 1)
    row = (corner - column) // TILE_W
    rows = [
        bilinear[...].astype(F32),
        row.astype(F32),
        column.astype(F32),
        jnp.zeros((2, slots), F32),
        rounded(lower),
        lower - rounded(lower),
        rounded(upper),
        upper - rounded(upper),
    ]
    rows.append(jnp.zeros((LANES - 8 - 4 * npred, slots), F32))
    extra = jnp.concatenate(rows, axis=0).astype(BF16)
    out[:, channels:] = dot_dims(identity(slots, slots), extra, NT).astype(BF16)


def terms_kernel(got, out):
    slots, width = got.shape
    cap = out.shape[1]
    mine = (place((8, slots), 1) % cap == place((8, slots), 0)).astype(F32).astype(BF16)
    terms = dot(mine, got[:, width - LANES :])
    for peer in range(out.shape[0]):
        out[peer] = terms[:cap]


def spread_of(extra, columns):
    extra = extra.astype(F32)
    corner = (extra[:, 4:5] * TILE_W + extra[:, 5:6]).astype(I32)
    delta = place((extra.shape[0], columns), 1) - corner
    spread = jnp.zeros(delta.shape, F32)
    for k, offset in enumerate((0, 1, TILE_W, TILE_W + 1)):
        spread = jnp.where(delta == offset, extra[:, k : k + 1], spread)
    return spread.astype(BF16)


def profile_kernel(got, state, out):
    width = got.shape[1]
    spread = spread_of(got[:, width - LANES :], state.shape[0])
    out[...] = dot(spread, state[...]).astype(BF16)


def forward(profile, w_in, b_in, w_mid, b_mid):
    h1 = jnp.tanh(dot(profile, w_in[...]) + b_in[...]).astype(BF16)
    h2 = jnp.tanh(dot(h1, w_mid[...]) + b_mid[...]).astype(BF16)
    return h1, h2


def grad_kernel(got, profile, w_in, b_in, w_mid, b_mid, w_out, out):
    width = got.shape[1]
    h1, h2 = forward(profile[...], w_in, b_in, w_mid, b_mid)
    h2, h1 = h2.astype(F32), h1.astype(F32)
    g2 = dot_dims(got[:, : width - LANES], w_out[...], NT)
    g2 = (g2 * (1.0 - h2 * h2)).astype(BF16)
    g1 = dot_dims(g2, w_mid[...], NT)
    g1 = (g1 * (1.0 - h1 * h1)).astype(BF16)
    dprofile = dot_dims(g1, w_in[...], NT).astype(BF16)
    spread = spread_of(got[:, width - LANES :], out.shape[0])
    out[...] = dot_dims(spread, dprofile, TN)


def reply_kernel(scale, npred, profile, terms, out):
    slots, feat = profile.shape
    cap = terms.shape[1]
    total = terms[0]
    for peer in range(1, terms.shape[0]):
        total = total + terms[peer]
    total = jnp.concatenate([total, jnp.zeros((8 - cap, LANES), F32)], axis=0)
    joined = (total + pltpu.roll(total, LANES - npred, 1)) * scale
    high = rounded(joined)
    low = pltpu.roll(joined - high, npred, 1)
    lanes = place((8, LANES), 1)
    is_high = ((lanes >= 8) & (lanes < 8 + npred)) | (
        (lanes >= 8 + 2 * npred) & (lanes < 8 + 3 * npred)
    )
    tail = jnp.where(is_high, high, low)
    which = (place((slots, 8), 0) % cap == place((slots, 8), 1)).astype(F32).astype(BF16)
    out[:, :feat] = profile[...]
    out[:, feat:] = dot(which, tail.astype(BF16)).astype(BF16)


def radiance_kernel(back, w_in, b_in, w_mid, b_mid, w_out, b_out, radiance, bias_grad):
    slots = back.shape[0]
    npred, channels = bias_grad.shape
    feat = w_in.shape[0]
    _, h2 = forward(back[:, :feat], w_in, b_in, w_mid, b_mid)
    radiance[...] = (dot(h2, w_out[...]) + b_out[...]).astype(BF16)
    turned = dot_dims(back[:, feat:], identity(slots, channels), TN)
    at = lambda k: turned[8 + k * npred : 8 + (k + 1) * npred]
    lower, upper = at(0) + at(1), at(2) + at(3)
    bias_grad[:, :LANES] = lower[:, :LANES]
    lanes = place((npred, channels - LANES), 1)
    bias_grad[:, LANES:] = jnp.where(
        lanes < slots - LANES, lower[:, LANES:], upper[:, : channels - LANES]
    )


def call(kernel, out, *args, flops=0, touched=0):
    return pl.pallas_call(
        kernel,
        out_shape=out,
        in_specs=[pl.BlockSpec(memory_space=pltpu.VMEM)] * len(args),
        out_specs=jax.tree.map(lambda _: pl.BlockSpec(memory_space=pltpu.VMEM), out),
        compiler_params=pltpu.CompilerParams(vmem_limit_bytes=GRANT),
        cost_estimate=pl.CostEstimate(flops=flops, bytes_accessed=touched, transcendentals=0),
    )(*args)


def on_device(
    state, departures, stencil, bilinear, counts, predictors, w_in, b_in, w_mid, b_mid, w_out, b_out
):
    slots, channels = departures.shape
    columns, feat = state.shape
    npred = predictors.shape[0]
    peers, rows = lax.axis_size("tx"), lax.axis_size("ty")
    cap = slots // peers
    scale = 1.0 / math.sqrt(slots * peers * rows)
    b_in, b_mid, b_out = b_in[None], b_mid[None], b_out[None]
    shape = jax.ShapeDtypeStruct

    sent = call(
        pack_kernel,
        shape((slots, channels + LANES), BF16),
        departures,
        stencil.T,
        bilinear.T,
        counts[None],
        predictors,
        flops=40_000_000,
        touched=300_000,
    )
    got = exchange(sent.reshape(peers, cap, -1), "tx").reshape(slots, -1)
    terms = call(terms_kernel, shape((rows, cap, LANES), F32), got, flops=1_000_000, touched=200_000)
    terms = exchange(terms, "ty")
    profile = call(
        profile_kernel, shape((slots, feat), BF16), got, state, flops=50_000_000, touched=500_000
    )
    reply = call(
        functools.partial(reply_kernel, scale, npred),
        shape((slots, feat + LANES), BF16),
        profile,
        terms,
        flops=1_000_000,
        touched=200_000,
    )
    back = exchange(reply.reshape(peers, cap, -1), "tx").reshape(slots, -1)
    state_grad = call(
        grad_kernel,
        shape((columns, feat), F32),
        got,
        profile,
        w_in,
        b_in,
        w_mid,
        b_mid,
        w_out,
        flops=400_000_000,
        touched=2_000_000,
    )
    radiance, bias_grad = call(
        radiance_kernel,
        (shape((slots, channels), BF16), shape((npred, channels), F32)),
        back,
        w_in,
        b_in,
        w_mid,
        b_mid,
        w_out,
        b_out,
        flops=200_000_000,
        touched=1_000_000,
    )
    return (radiance, state_grad, bias_grad)


def solution(mesh):
    both = P(("tx", "ty"), None)
    placed = (both, both, both, both, P(("tx", "ty")), P(None, ("tx", "ty"))) + (P(),) * 6
    return jax.shard_map(
        on_device,
        mesh=mesh,
        in_specs=placed,
        out_specs=(both, both, P()),
        check_vma=False,
    )
```

```python
import functools
import math

import jax
import jax.numpy as jnp
from jax import lax
from jax.experimental import pallas as pl
from jax.experimental.pallas import tpu as pltpu
from jax.sharding import PartitionSpec as P

F32, BF16, I32 = jnp.float32, jnp.bfloat16, jnp.int32
NT = (((1,), (1,)), ((), ()))
TN = (((0,), (0,)), ((), ()))
TILE_W = 32
LANES = 128
GRANT = 40 * 1024 * 1024


def exchange(block, axis):
    return lax.all_to_all(block, axis, split_axis=0, concat_axis=0, tiled=True)


def dot(a, b):
    return jnp.dot(a, b, preferred_element_type=F32)


def dot_dims(a, b, dims):
    return lax.dot_general(a, b, dims, preferred_element_type=F32)


def place(shape, dim):
    return lax.broadcasted_iota(I32, shape, dim)


def identity(rows, columns):
    shape = (rows, columns)
    return (place(shape, 0) == place(shape, 1)).astype(F32).astype(BF16)


def rounded(x):
    return x.astype(BF16).astype(F32)


def pack_kernel(
    departures_hbm, stencil_hbm, bilinear_hbm, counts_hbm, predictors_hbm, out, shared,
    departures, stencil, bilinear, counts, predictors, arrived
):
    pairs = (
        (counts_hbm, counts),
        (departures_hbm, departures),
        (predictors_hbm, predictors),
        (stencil_hbm, stencil),
        (bilinear_hbm, bilinear),
    )
    copies = [
        pltpu.make_async_copy(source, target, arrived.at[k])
        for k, (source, target) in enumerate(pairs)
    ]
    for copy in copies:
        copy.start()
    slots, channels = departures.shape
    peers = counts.shape[1]
    cap = slots // peers
    npred = predictors.shape[0]
    holds = (place((slots, peers), 0) // cap == place((slots, peers), 1)).astype(F32).astype(BF16)
    turn = identity(slots, slots)
    for copy in copies:
        copy.wait()
    counted = jnp.broadcast_to(counts[...].astype(F32), (8, peers)).astype(BF16)
    count_of = dot_dims(holds, counted, NT)[:, 0:1]
    live = (place((slots, 1), 0) % cap).astype(F32) < count_of
    dy = jnp.where(live, departures[...].astype(F32), 0.0).astype(BF16)
    out[:, :channels] = dy

    pred = predictors[...]
    part0 = rounded(pred)
    part1 = rounded(pred - part0)
    part2 = pred - part0 - part1
    thirds = dot(jnp.concatenate([part0, part1, part2], axis=0).astype(BF16), dy)
    partial = thirds[:npred] + thirds[npred : 2 * npred] + thirds[2 * npred :]
    for peer in range(shared.shape[0]):
        shared[peer] = partial

    corner = stencil[0:1, :]
    column = jnp.bitwise_and(corner, TILE_W - 1)
    row = (corner - column) // TILE_W
    rows = [bilinear[...].astype(F32), row.astype(F32), column.astype(F32)]
    rows.append(jnp.zeros((LANES - 6, slots), F32))
    extra = jnp.concatenate(rows, axis=0).astype(BF16)
    out[:, channels:] = dot_dims(turn, extra, NT).astype(BF16)


def terms_kernel(packed, shared, out):
    slots, width = packed.shape
    npred, channels = shared.shape[1:]
    total = shared[0]
    for peer in range(1, shared.shape[0]):
        total = total + shared[peer]
    rest = channels - LANES
    upper = jnp.where(place((npred, rest), 1) >= slots - LANES, total[:, LANES:], 0.0)
    upper = jnp.concatenate([upper, jnp.zeros((npred, slots - rest), F32)], axis=1)
    lower = total[:, :slots]
    rows = [
        jnp.zeros((8, slots), F32),
        rounded(lower),
        lower - rounded(lower),
        rounded(upper),
        upper - rounded(upper),
        jnp.zeros((LANES - 8 - 4 * npred, slots), F32),
    ]
    rows = jnp.concatenate(rows, axis=0).astype(BF16)
    out[:, :channels] = packed[:, :channels]
    extra = dot_dims(identity(slots, slots), rows, NT)
    out[:, channels:] = (packed[:, channels:].astype(F32) + extra).astype(BF16)


def spread_of(extra, columns):
    extra = extra.astype(F32)
    corner = (extra[:, 4:5] * TILE_W + extra[:, 5:6]).astype(I32)
    delta = place((extra.shape[0], columns), 1) - corner
    spread = jnp.zeros(delta.shape, F32)
    for k, offset in enumerate((0, 1, TILE_W, TILE_W + 1)):
        spread = jnp.where(delta == offset, extra[:, k : k + 1], spread)
    return spread.astype(BF16)


def reply_kernel(scale, npred, cap, got, state, out):
    slots, width = got.shape
    feat = state.shape[1]
    extra = got[:, width - LANES :]
    mine = (place((8, slots), 1) % cap == place((8, slots), 0)).astype(F32).astype(BF16)
    total = dot(mine, extra)
    joined = (total + pltpu.roll(total, LANES - npred, 1)) * scale
    high = rounded(joined)
    low = pltpu.roll(joined - high, npred, 1)
    lanes = place((8, LANES), 1)
    is_high = ((lanes >= 8) & (lanes < 8 + npred)) | (
        (lanes >= 8 + 2 * npred) & (lanes < 8 + 3 * npred)
    )
    tail = jnp.where(is_high, high, low).astype(BF16)
    which = (place((slots, 8), 0) % cap == place((slots, 8), 1)).astype(F32).astype(BF16)
    out[:, feat:] = dot(which, tail).astype(BF16)
    spread = spread_of(extra, state.shape[0])
    out[:, :feat] = dot(spread, state[...]).astype(BF16)


def forward(profile, w_in, b_in, w_mid, b_mid):
    h1 = jnp.tanh(dot(profile, w_in[...]) + b_in[...]).astype(BF16)
    h2 = jnp.tanh(dot(h1, w_mid[...]) + b_mid[...]).astype(BF16)
    return h1, h2


def grad_kernel(got, reply, w_in, b_in, w_mid, b_mid, w_out, b_out, out, b_kept):
    width = got.shape[1]
    b_kept[...] = b_out[...]
    h1, h2 = forward(reply[:, : w_in.shape[0]], w_in, b_in, w_mid, b_mid)
    h2, h1 = h2.astype(F32), h1.astype(F32)
    g2 = dot_dims(got[:, : width - LANES], w_out[...], NT)
    g2 = (g2 * (1.0 - h2 * h2)).astype(BF16)
    g1 = dot_dims(g2, w_mid[...], NT)
    g1 = (g1 * (1.0 - h1 * h1)).astype(BF16)
    dprofile = dot_dims(g1, w_in[...], NT).astype(BF16)
    spread = spread_of(got[:, width - LANES :], out.shape[0])
    out[...] = dot_dims(spread, dprofile, TN)


def radiance_kernel(back, w_in, b_in, w_mid, b_mid, w_out, b_out, radiance, bias_grad):
    slots = back.shape[0]
    npred, channels = bias_grad.shape
    feat = w_in.shape[0]
    _, h2 = forward(back[:, :feat], w_in, b_in, w_mid, b_mid)
    radiance[...] = (dot(h2, w_out[...]) + b_out[...]).astype(BF16)
    turned = dot_dims(back[:, feat:], identity(slots, channels), TN)
    at = lambda k: turned[8 + k * npred : 8 + (k + 1) * npred]
    lower, upper = at(0) + at(1), at(2) + at(3)
    bias_grad[:, :LANES] = lower[:, :LANES]
    lanes = place((npred, channels - LANES), 1)
    bias_grad[:, LANES:] = jnp.where(
        lanes < slots - LANES, lower[:, LANES:], upper[:, : channels - LANES]
    )


def call(kernel, out, *args, flops=0, touched=0, space=pltpu.VMEM, scratch=(), grant=GRANT):
    return pl.pallas_call(
        kernel,
        out_shape=out,
        in_specs=[pl.BlockSpec(memory_space=space)] * len(args),
        out_specs=jax.tree.map(lambda _: pl.BlockSpec(memory_space=pltpu.VMEM), out),
        scratch_shapes=scratch,
        compiler_params=pltpu.CompilerParams(vmem_limit_bytes=grant),
        cost_estimate=pl.CostEstimate(flops=flops, bytes_accessed=touched, transcendentals=0),
    )(*args)


def on_device(
    state, departures, stencil, bilinear, counts, predictors, w_in, b_in, w_mid, b_mid, w_out, b_out
):
    slots, channels = departures.shape
    columns, feat = state.shape
    npred = predictors.shape[0]
    peers, rows = lax.axis_size("tx"), lax.axis_size("ty")
    cap = slots // peers
    scale = 1.0 / math.sqrt(slots * peers * rows)
    b_in, b_mid, b_out = b_in[None], b_mid[None], b_out[None]
    shape = jax.ShapeDtypeStruct

    inputs = (departures, stencil.T, bilinear.T, counts[None], predictors)
    packed, shared = call(
        pack_kernel,
        (shape((slots, channels + LANES), BF16), shape((rows, npred, channels), F32)),
        *inputs,
        flops=40_000_000,
        touched=300_000,
        space=pl.ANY,
        scratch=[pltpu.VMEM(a.shape, a.dtype) for a in inputs]
        + [pltpu.SemaphoreType.DMA((len(inputs),))],
        grant=60 * 1024 * 1024,
    )
    shared = exchange(shared, "ty")
    sent = call(
        terms_kernel,
        shape((slots, channels + LANES), BF16),
        packed,
        shared,
        flops=20_000_000,
        touched=300_000,
    )
    got = exchange(sent.reshape(peers, cap, -1), "tx").reshape(slots, -1)
    reply = call(
        functools.partial(reply_kernel, scale, npred, cap),
        shape((slots, feat + LANES), BF16),
        got,
        state,
        flops=50_000_000,
        touched=500_000,
    )
    back = exchange(reply.reshape(peers, cap, -1), "tx").reshape(slots, -1)
    state_grad, b_out = call(
        grad_kernel,
        (shape((columns, feat), F32), shape((1, channels), F32)),
        got,
        reply,
        w_in,
        b_in,
        w_mid,
        b_mid,
        w_out,
        b_out,
        flops=400_000_000,
        touched=2_000_000,
    )
    radiance, bias_grad = call(
        radiance_kernel,
        (shape((slots, channels), BF16), shape((npred, channels), F32)),
        back,
        w_in,
        b_in,
        w_mid,
        b_mid,
        w_out,
        b_out,
        flops=200_000_000,
        touched=1_000_000,
    )
    return (radiance, state_grad, bias_grad)


def solution(mesh):
    both = P(("tx", "ty"), None)
    placed = (both, both, both, both, P(("tx", "ty")), P(None, ("tx", "ty"))) + (P(),) * 6
    return jax.shard_map(
        on_device,
        mesh=mesh,
        in_specs=placed,
        out_specs=(both, both, P()),
        check_vma=False,
    )
```

```python
import functools
import math

import jax
import jax.numpy as jnp
from jax import lax
from jax.experimental import pallas as pl
from jax.experimental.pallas import tpu as pltpu
from jax.sharding import PartitionSpec as P

F32, BF16, I32 = jnp.float32, jnp.bfloat16, jnp.int32
NT = (((1,), (1,)), ((), ()))
TN = (((0,), (0,)), ((), ()))
TILE_W = 32
LANES = 128
GRANT = 40 * 1024 * 1024
PACK_GRANT = 60 * 1024 * 1024


def exchange(block, axis):
    return lax.all_to_all(block, axis, split_axis=0, concat_axis=0, tiled=True)


def dot(a, b):
    return jnp.dot(a, b, preferred_element_type=F32)


def dot_dims(a, b, dims):
    return lax.dot_general(a, b, dims, preferred_element_type=F32)


def place(shape, dim):
    return lax.broadcasted_iota(I32, shape, dim)


def identity(rows, columns):
    shape = (rows, columns)
    return (place(shape, 0) == place(shape, 1)).astype(F32).astype(BF16)


def rounded(x):
    return x.astype(BF16).astype(F32)


def pack_kernel(
    departures_hbm, stencil_hbm, bilinear_hbm, counts_hbm, predictors_hbm, out, masked,
    departures, stencil, bilinear, counts, predictors, arrived
):
    pairs = (
        (counts_hbm, counts),
        (departures_hbm, departures),
        (predictors_hbm, predictors),
        (stencil_hbm, stencil),
        (bilinear_hbm, bilinear),
    )
    copies = [
        pltpu.make_async_copy(source, target, arrived.at[k])
        for k, (source, target) in enumerate(pairs)
    ]
    for copy in copies:
        copy.start()
    slots, channels = departures.shape
    peers = counts.shape[1]
    cap = slots // peers
    npred = predictors.shape[0]
    holds = (place((slots, peers), 0) // cap == place((slots, peers), 1)).astype(F32).astype(BF16)
    turn = identity(slots, slots)
    for copy in copies:
        copy.wait()
    counted = jnp.broadcast_to(counts[...].astype(F32), (8, peers)).astype(BF16)
    count_of = dot_dims(holds, counted, NT)[:, 0:1]
    live = (place((slots, 1), 0) % cap).astype(F32) < count_of
    dy = jnp.where(live, departures[...].astype(F32), 0.0).astype(BF16)
    masked[...] = dy

    pred = predictors[...]
    part0 = rounded(pred)
    part1 = rounded(pred - part0)
    part2 = pred - part0 - part1
    thirds = dot(jnp.concatenate([part0, part1, part2], axis=0).astype(BF16), dy)
    partial = thirds[:npred] + thirds[npred : 2 * npred] + thirds[2 * npred :]
    slot = place((slots, npred), 0) % (2 * cap) * 2
    which = place((slots, npred), 1)
    partial = partial.astype(BF16)
    for k in range(2):
        chosen = (which == slot + k).astype(F32).astype(BF16)
        out[:, LANES + k * channels : LANES + (k + 1) * channels] = dot(chosen, partial).astype(BF16)

    corner = stencil[0:1, :]
    column = jnp.bitwise_and(corner, TILE_W - 1)
    row = (corner - column) // TILE_W
    rows = [bilinear[...].astype(F32), row.astype(F32), column.astype(F32)]
    rows.append(jnp.zeros((LANES - 6, slots), F32))
    extra = jnp.concatenate(rows, axis=0).astype(BF16)
    out[:, :LANES] = dot_dims(turn, extra, NT).astype(BF16)


def spread_of(extra, columns):
    extra = extra.astype(F32)
    corner = (extra[:, 4:5] * TILE_W + extra[:, 5:6]).astype(I32)
    delta = place((extra.shape[0], columns), 1) - corner
    spread = jnp.zeros(delta.shape, F32)
    for k, offset in enumerate((0, 1, TILE_W, TILE_W + 1)):
        spread = jnp.where(delta == offset, extra[:, k : k + 1], spread)
    return spread.astype(BF16)


def reply_kernel(cap, got, dy, state, out, terms):
    slots = got.shape[0]
    feat = state.shape[1]
    mine = (place((8, slots), 1) % cap == place((8, slots), 0)).astype(F32).astype(BF16)
    terms[...] = dot(mine, got[:, LANES:])
    spread = spread_of(got[:, :LANES], state.shape[0])
    out[:, :feat] = dot(spread, state[...]).astype(BF16)
    out[:, feat:] = dy[...]


def forward(profile, w_in, b_in, w_mid, b_mid):
    h1 = jnp.tanh(dot(profile, w_in[...]) + b_in[...]).astype(BF16)
    h2 = jnp.tanh(dot(h1, w_mid[...]) + b_mid[...]).astype(BF16)
    return h1, h2


def hidden_kernel(reply, w_in, b_in, w_mid, b_mid, b_out, h1, h2, b_kept):
    b_kept[...] = b_out[...]
    h1[...], h2[...] = forward(reply[:, : w_in.shape[0]], w_in, b_in, w_mid, b_mid)


def final_kernel(
    scale, back, got, h1, h2, even, odd, w_in, b_in, w_mid, b_mid, w_out, b_out,
    state_grad, radiance, bias_grad
):
    feat = w_in.shape[0]
    channels = bias_grad.shape[1]
    h2f, h1f = h2[...].astype(F32), h1[...].astype(F32)
    g2 = dot_dims(back[:, feat:], w_out[...], NT)
    g2 = (g2 * (1.0 - h2f * h2f)).astype(BF16)
    g1 = dot_dims(g2, w_mid[...], NT)
    g1 = (g1 * (1.0 - h1f * h1f)).astype(BF16)
    dprofile = dot_dims(g1, w_in[...], NT).astype(BF16)
    spread = spread_of(got[:, :LANES], state_grad.shape[0])
    state_grad[...] = dot_dims(spread, dprofile, TN)

    _, last = forward(back[:, :feat], w_in, b_in, w_mid, b_mid)
    radiance[...] = (dot(last, w_out[...]) + b_out[...]).astype(BF16)

    for k, half in enumerate((even, odd)):
        for j in range(2):
            for e in range(2):
                row = 4 * k + 2 * j + e
                bias_grad[row : row + 1, :] = (
                    half[j : j + 1, e * channels : (e + 1) * channels] * scale
                )


def call(kernel, out, *args, flops=0, touched=0, space=pltpu.VMEM, scratch=(), grant=GRANT):
    return pl.pallas_call(
        kernel,
        out_shape=out,
        in_specs=[pl.BlockSpec(memory_space=space)] * len(args),
        out_specs=jax.tree.map(lambda _: pl.BlockSpec(memory_space=pltpu.VMEM), out),
        scratch_shapes=scratch,
        compiler_params=pltpu.CompilerParams(vmem_limit_bytes=grant),
        cost_estimate=pl.CostEstimate(flops=flops, bytes_accessed=touched, transcendentals=0),
    )(*args)


def on_device(
    state, departures, stencil, bilinear, counts, predictors, w_in, b_in, w_mid, b_mid, w_out, b_out
):
    slots, channels = departures.shape
    columns, feat = state.shape
    npred = predictors.shape[0]
    peers, rows = lax.axis_size("tx"), lax.axis_size("ty")
    cap = slots // peers
    scale = 1.0 / math.sqrt(slots * peers * rows)
    b_in, b_mid, b_out = b_in[None], b_mid[None], b_out[None]
    shape = jax.ShapeDtypeStruct

    inputs = (departures, stencil.T, bilinear.T, counts[None], predictors)
    packed, dy = call(
        pack_kernel,
        (shape((slots, LANES + 2 * channels), BF16), shape((slots, channels), BF16)),
        *inputs,
        flops=40_000_000,
        touched=300_000,
        space=pl.ANY,
        scratch=[pltpu.VMEM(a.shape, a.dtype) for a in inputs]
        + [pltpu.SemaphoreType.DMA((len(inputs),))],
        grant=PACK_GRANT,
    )
    got = exchange(packed.reshape(peers, cap, -1), "tx").reshape(slots, -1)
    reply, terms = call(
        functools.partial(reply_kernel, cap),
        (shape((slots, feat + channels), BF16), shape((8, 2 * channels), F32)),
        got,
        dy,
        state,
        flops=50_000_000,
        touched=500_000,
    )
    back = exchange(reply.reshape(peers, cap, -1), "tx").reshape(slots, -1)
    h1, h2, b_out = call(
        hidden_kernel,
        (shape((slots, w_in.shape[1]), BF16),) * 2 + (shape((1, channels), F32),),
        reply,
        w_in,
        b_in,
        w_mid,
        b_mid,
        b_out,
        flops=130_000_000,
        touched=1_000_000,
    )
    terms = lax.psum(terms[:cap], "ty")
    other = lax.ppermute(terms, "tx", [(a, a ^ 1) for a in range(peers)])
    is_even = lax.axis_index("tx") % 2 == 0
    even = jnp.where(is_even, terms, other)
    odd = jnp.where(is_even, other, terms)
    state_grad, radiance, bias_grad = call(
        functools.partial(final_kernel, scale),
        (
            shape((columns, feat), F32),
            shape((slots, channels), BF16),
            shape((npred, channels), F32),
        ),
        back,
        got,
        h1,
        h2,
        even,
        odd,
        w_in,
        b_in,
        w_mid,
        b_mid,
        w_out,
        b_out,
        flops=400_000_000,
        touched=2_000_000,
    )
    return (radiance, state_grad, bias_grad)


def solution(mesh):
    both = P(("tx", "ty"), None)
    placed = (both, both, both, both, P(("tx", "ty")), P(None, ("tx", "ty"))) + (P(),) * 6
    return jax.shard_map(
        on_device,
        mesh=mesh,
        in_specs=placed,
        out_specs=(both, both, P()),
        check_vma=False,
    )
```

```python
import functools
import math

import jax
import jax.numpy as jnp
from jax import lax
from jax.experimental import pallas as pl
from jax.experimental.pallas import tpu as pltpu
from jax.sharding import PartitionSpec as P

F32, BF16, I32 = jnp.float32, jnp.bfloat16, jnp.int32
NT = (((1,), (1,)), ((), ()))
TN = (((0,), (0,)), ((), ()))
TILE_W = 32
LANES = 128
GRANT = 40 * 1024 * 1024
PACK_GRANT = 60 * 1024 * 1024


def exchange(block, axis):
    return lax.all_to_all(block, axis, split_axis=0, concat_axis=0, tiled=True)


def dot(a, b):
    return jnp.dot(a, b, preferred_element_type=F32)


def dot_dims(a, b, dims):
    return lax.dot_general(a, b, dims, preferred_element_type=F32)


def place(shape, dim):
    return lax.broadcasted_iota(I32, shape, dim)


def identity(rows, columns):
    shape = (rows, columns)
    return (place(shape, 0) == place(shape, 1)).astype(F32).astype(BF16)


def rounded(x):
    return x.astype(BF16).astype(F32)


def masked_by(departures, counts):
    slots, peers = departures.shape[0], counts.shape[1]
    cap = slots // peers
    holds = (place((slots, peers), 0) // cap == place((slots, peers), 1)).astype(F32).astype(BF16)
    counted = jnp.broadcast_to(counts[...].astype(F32), (8, peers)).astype(BF16)
    count_of = dot_dims(holds, counted, NT)[:, 0:1]
    live = (place((slots, 1), 0) % cap).astype(F32) < count_of
    return jnp.where(live, departures[...].astype(F32), 0.0).astype(BF16)


def keep_kernel(state, departures, counts, state_kept, dy):
    state_kept[...] = state[...]
    dy[...] = masked_by(departures, counts)


def pack_kernel(
    departures_hbm, stencil_hbm, bilinear_hbm, counts_hbm, predictors_hbm, out,
    departures, stencil, bilinear, counts, predictors, arrived
):
    pairs = (
        (counts_hbm, counts),
        (departures_hbm, departures),
        (predictors_hbm, predictors),
        (stencil_hbm, stencil),
        (bilinear_hbm, bilinear),
    )
    copies = [
        pltpu.make_async_copy(source, target, arrived.at[k])
        for k, (source, target) in enumerate(pairs)
    ]
    for copy in copies:
        copy.start()
    slots, channels = departures.shape
    peers = counts.shape[1]
    cap = slots // peers
    npred = predictors.shape[0]
    turn = identity(slots, slots)
    for copy in copies:
        copy.wait()
    dy = masked_by(departures, counts)

    pred = predictors[...]
    part0 = rounded(pred)
    part1 = rounded(pred - part0)
    part2 = pred - part0 - part1
    thirds = dot(jnp.concatenate([part0, part1, part2], axis=0).astype(BF16), dy)
    partial = thirds[:npred] + thirds[npred : 2 * npred] + thirds[2 * npred :]
    slot = place((slots, npred), 0) % (2 * cap) * 2
    which = place((slots, npred), 1)
    partial = partial.astype(BF16)
    for k in range(2):
        chosen = (which == slot + k).astype(F32).astype(BF16)
        out[:, :, LANES + k * channels : LANES + (k + 1) * channels] = (
            dot(chosen, partial).astype(BF16).reshape(peers, cap, channels)
        )

    corner = stencil[0:1, :]
    column = jnp.bitwise_and(corner, TILE_W - 1)
    row = (corner - column) // TILE_W
    rows = [bilinear[...].astype(F32), row.astype(F32), column.astype(F32)]
    rows.append(jnp.zeros((LANES - 6, slots), F32))
    extra = jnp.concatenate(rows, axis=0).astype(BF16)
    out[:, :, :LANES] = dot_dims(turn, extra, NT).astype(BF16).reshape(peers, cap, LANES)


def spread_of(extra, columns):
    extra = extra.astype(F32)
    corner = (extra[:, 4:5] * TILE_W + extra[:, 5:6]).astype(I32)
    delta = place((extra.shape[0], columns), 1) - corner
    spread = jnp.zeros(delta.shape, F32)
    for k, offset in enumerate((0, 1, TILE_W, TILE_W + 1)):
        spread = jnp.where(delta == offset, extra[:, k : k + 1], spread)
    return spread.astype(BF16)


def reply_kernel(cap, got, dy, state, out, terms, kept):
    slots = got.shape[0]
    feat = state.shape[1]
    mine = (place((8, slots), 1) % cap == place((8, slots), 0)).astype(F32).astype(BF16)
    terms[...] = dot(mine, got[:, LANES:])
    spread = spread_of(got[:, :LANES], state.shape[0])
    shape = out.shape[:2]
    profile = dot(spread, state[...]).astype(BF16)
    kept[...] = profile
    out[:, :, :feat] = profile.reshape(*shape, feat)
    out[:, :, feat:] = dy[...].reshape(*shape, dy.shape[1])


def forward(profile, w_in, b_in, w_mid, b_mid):
    h1 = jnp.tanh(dot(profile, w_in[...]) + b_in[...]).astype(BF16)
    h2 = jnp.tanh(dot(h1, w_mid[...]) + b_mid[...]).astype(BF16)
    return h1, h2


def hidden_kernel(profile, w_in, b_in, w_mid, b_mid, w_out, b_out, h1, h2, b_kept):
    b_kept[...] = b_out[...]
    h1[...], h2[...] = forward(profile[...], w_in, b_in, w_mid, b_mid)


def final_kernel(
    scale, back, got, h1, h2, even, odd, w_in, b_in, w_mid, b_mid, w_out, b_out,
    state_grad, radiance, bias_grad
):
    feat = w_in.shape[0]
    channels = bias_grad.shape[1]
    h2f, h1f = h2[...].astype(F32), h1[...].astype(F32)
    g2 = dot_dims(back[:, feat:], w_out[...], NT)
    g2 = (g2 * (1.0 - h2f * h2f)).astype(BF16)
    g1 = dot_dims(g2, w_mid[...], NT)
    g1 = (g1 * (1.0 - h1f * h1f)).astype(BF16)
    dprofile = dot_dims(g1, w_in[...], NT).astype(BF16)
    spread = spread_of(got[:, :LANES], state_grad.shape[0])
    state_grad[...] = dot_dims(spread, dprofile, TN)

    _, last = forward(back[:, :feat], w_in, b_in, w_mid, b_mid)
    radiance[...] = (dot(last, w_out[...]) + b_out[...]).astype(BF16)

    for k, half in enumerate((even, odd)):
        for j in range(2):
            for e in range(2):
                row = 4 * k + 2 * j + e
                bias_grad[row : row + 1, :] = (
                    half[j : j + 1, e * channels : (e + 1) * channels] * scale
                )


def call(kernel, out, *args, flops=0, touched=0, space=pltpu.VMEM, scratch=(), grant=GRANT):
    return pl.pallas_call(
        kernel,
        out_shape=out,
        in_specs=[pl.BlockSpec(memory_space=space)] * len(args),
        out_specs=jax.tree.map(lambda _: pl.BlockSpec(memory_space=pltpu.VMEM), out),
        scratch_shapes=scratch,
        compiler_params=pltpu.CompilerParams(vmem_limit_bytes=grant),
        cost_estimate=pl.CostEstimate(flops=flops, bytes_accessed=touched, transcendentals=0),
    )(*args)


def on_device(
    state, departures, stencil, bilinear, counts, predictors, w_in, b_in, w_mid, b_mid, w_out, b_out
):
    slots, channels = departures.shape
    columns, feat = state.shape
    npred = predictors.shape[0]
    peers, rows = lax.axis_size("tx"), lax.axis_size("ty")
    cap = slots // peers
    scale = 1.0 / math.sqrt(slots * peers * rows)
    b_in, b_mid, b_out = b_in[None], b_mid[None], b_out[None]
    shape = jax.ShapeDtypeStruct

    inputs = (departures, stencil.T, bilinear.T, counts[None], predictors)
    packed = call(
        pack_kernel,
        shape((peers, cap, LANES + 2 * channels), BF16),
        *inputs,
        flops=40_000_000,
        touched=300_000,
        space=pl.ANY,
        scratch=[pltpu.VMEM(a.shape, a.dtype) for a in inputs]
        + [pltpu.SemaphoreType.DMA((len(inputs),))],
        grant=PACK_GRANT,
    )
    state, dy = call(
        keep_kernel,
        (shape(state.shape, BF16), shape(departures.shape, BF16)),
        state,
        departures,
        counts[None],
        flops=2_000_000_000,
        touched=2_000_000,
    )
    got = exchange(packed, "tx").reshape(slots, -1)
    reply, terms, profile = call(
        functools.partial(reply_kernel, cap),
        (
            shape((peers, cap, feat + channels), BF16),
            shape((8, 2 * channels), F32),
            shape((slots, feat), BF16),
        ),
        got,
        dy,
        state,
        flops=50_000_000,
        touched=500_000,
    )
    back = exchange(reply, "tx").reshape(slots, -1)
    h1, h2, b_out = call(
        hidden_kernel,
        (shape((slots, w_in.shape[1]), BF16),) * 2 + (shape((1, channels), F32),),
        profile,
        w_in,
        b_in,
        w_mid,
        b_mid,
        w_out,
        b_out,
        flops=130_000_000,
        touched=1_000_000,
    )
    terms = terms[:cap]
    for step in (1 << k for k in range((rows - 1).bit_length())):
        terms = terms + lax.ppermute(terms, "ty", [(b, b ^ step) for b in range(rows)])
    other = lax.ppermute(terms, "tx", [(a, a ^ 1) for a in range(peers)])
    is_even = lax.axis_index("tx") % 2 == 0
    even = jnp.where(is_even, terms, other)
    odd = jnp.where(is_even, other, terms)
    state_grad, radiance, bias_grad = call(
        functools.partial(final_kernel, scale),
        (
            shape((columns, feat), F32),
            shape((slots, channels), BF16),
            shape((npred, channels), F32),
        ),
        back,
        got,
        h1,
        h2,
        even,
        odd,
        w_in,
        b_in,
        w_mid,
        b_mid,
        w_out,
        b_out,
        flops=400_000_000,
        touched=2_000_000,
    )
    return (radiance, state_grad, bias_grad)


def solution(mesh):
    both = P(("tx", "ty"), None)
    placed = (both, both, both, both, P(("tx", "ty")), P(None, ("tx", "ty"))) + (P(),) * 6
    return jax.shard_map(
        on_device,
        mesh=mesh,
        in_specs=placed,
        out_specs=(both, both, P()),
        check_vma=False,
    )
```

```python
import functools
import math

import jax
import jax.numpy as jnp
from jax import lax
from jax.experimental import pallas as pl
from jax.experimental.pallas import tpu as pltpu
from jax.sharding import PartitionSpec as P

F32, BF16, I32 = jnp.float32, jnp.bfloat16, jnp.int32
NT = (((1,), (1,)), ((), ()))
TN = (((0,), (0,)), ((), ()))
TILE_W = 32
LANES = 128
GRANT = 40 * 1024 * 1024
PACK_GRANT = 60 * 1024 * 1024


def exchange(block, axis):
    return lax.all_to_all(block, axis, split_axis=0, concat_axis=0, tiled=True)


def dot(a, b):
    return jnp.dot(a, b, preferred_element_type=F32)


def dot_dims(a, b, dims):
    return lax.dot_general(a, b, dims, preferred_element_type=F32)


def place(shape, dim):
    return lax.broadcasted_iota(I32, shape, dim)


def identity(rows, columns):
    shape = (rows, columns)
    return (place(shape, 0) == place(shape, 1)).astype(F32).astype(BF16)


def rounded(x):
    return x.astype(BF16).astype(F32)


def masked_by(departures, counts):
    slots, peers = departures.shape[0], counts.shape[1]
    cap = slots // peers
    holds = (place((slots, peers), 0) // cap == place((slots, peers), 1)).astype(F32).astype(BF16)
    counted = jnp.broadcast_to(counts[...].astype(F32), (8, peers)).astype(BF16)
    count_of = dot_dims(holds, counted, NT)[:, 0:1]
    live = (place((slots, 1), 0) % cap).astype(F32) < count_of
    return jnp.where(live, departures[...].astype(F32), 0.0).astype(BF16)


def keep_kernel(state, state_kept):
    state_kept[...] = state[...]


def pack_kernel(
    departures_hbm, stencil_hbm, bilinear_hbm, counts_hbm, predictors_hbm, out,
    departures, stencil, bilinear, counts, predictors, arrived
):
    pairs = (
        (counts_hbm, counts),
        (departures_hbm, departures),
        (predictors_hbm, predictors),
        (stencil_hbm, stencil),
        (bilinear_hbm, bilinear),
    )
    copies = [
        pltpu.make_async_copy(source, target, arrived.at[k])
        for k, (source, target) in enumerate(pairs)
    ]
    for copy in copies:
        copy.start()
    slots, channels = departures.shape
    peers = counts.shape[1]
    cap = slots // peers
    npred = predictors.shape[0]
    turn = identity(slots, slots)
    for copy in copies:
        copy.wait()
    dy = masked_by(departures, counts)
    out[:, :, :channels] = dy.reshape(peers, cap, channels)

    pred = predictors[...]
    part0 = rounded(pred)
    part1 = rounded(pred - part0)
    part2 = pred - part0 - part1
    thirds = dot(jnp.concatenate([part0, part1, part2], axis=0).astype(BF16), dy)
    partial = thirds[:npred] + thirds[npred : 2 * npred] + thirds[2 * npred :]
    rest = channels - LANES
    upper = jnp.where(place((npred, rest), 1) >= slots - LANES, partial[:, LANES:], 0.0)
    upper = jnp.concatenate([upper, jnp.zeros((npred, slots - rest), F32)], axis=1)
    lower = partial[:, :slots]
    corner = stencil[0:1, :]
    column = jnp.bitwise_and(corner, TILE_W - 1)
    row = (corner - column) // TILE_W
    rows = [
        bilinear[...].astype(F32),
        row.astype(F32),
        column.astype(F32),
        jnp.zeros((2, slots), F32),
        rounded(lower),
        lower - rounded(lower),
        rounded(upper),
        upper - rounded(upper),
        jnp.zeros((LANES - 8 - 4 * npred, slots), F32),
    ]
    extra = dot_dims(turn, jnp.concatenate(rows, axis=0).astype(BF16), NT).astype(BF16)
    out[:, :, channels:] = extra.reshape(peers, cap, LANES)


def spread_of(extra, columns):
    extra = extra.astype(F32)
    corner = (extra[:, 4:5] * TILE_W + extra[:, 5:6]).astype(I32)
    delta = place((extra.shape[0], columns), 1) - corner
    spread = jnp.zeros(delta.shape, F32)
    for k, offset in enumerate((0, 1, TILE_W, TILE_W + 1)):
        spread = jnp.where(delta == offset, extra[:, k : k + 1], spread)
    return spread.astype(BF16)


def reply_kernel(npred, got, state, out, kept):
    slots, width = got.shape
    peers, cap = out.shape[:2]
    feat = state.shape[1]
    extra = got[:, width - LANES :]
    mine = (place((8, slots), 1) % cap == place((8, slots), 0)).astype(F32).astype(BF16)
    total = dot(mine, extra)
    joined = total + pltpu.roll(total, LANES - npred, 1)
    high = rounded(joined)
    low = pltpu.roll(joined - high, npred, 1)
    lanes = place((8, LANES), 1)
    is_high = ((lanes >= 8) & (lanes < 8 + npred)) | (
        (lanes >= 8 + 2 * npred) & (lanes < 8 + 3 * npred)
    )
    tail = jnp.where(is_high, high, low).astype(BF16)
    for peer in range(peers):
        out[peer, :, feat:] = tail[:cap]
    spread = spread_of(extra, state.shape[0])
    profile = dot(spread, state[...]).astype(BF16)
    kept[...] = profile
    out[:, :, :feat] = profile.reshape(peers, cap, feat)


def forward(profile, w_in, b_in, w_mid, b_mid):
    h1 = jnp.tanh(dot(profile, w_in[...]) + b_in[...]).astype(BF16)
    h2 = jnp.tanh(dot(h1, w_mid[...]) + b_mid[...]).astype(BF16)
    return h1, h2


def grad_kernel(got, profile, w_in, b_in, w_mid, b_mid, w_out, b_out, out, b_kept):
    width = got.shape[1]
    b_kept[...] = b_out[...]
    h1, h2 = forward(profile[...], w_in, b_in, w_mid, b_mid)
    h2, h1 = h2.astype(F32), h1.astype(F32)
    g2 = dot_dims(got[:, : width - LANES], w_out[...], NT)
    g2 = (g2 * (1.0 - h2 * h2)).astype(BF16)
    g1 = dot_dims(g2, w_mid[...], NT)
    g1 = (g1 * (1.0 - h1 * h1)).astype(BF16)
    dprofile = dot_dims(g1, w_in[...], NT).astype(BF16)
    spread = spread_of(got[:, width - LANES :], out.shape[0])
    out[...] = dot_dims(spread, dprofile, TN)


def bias_kernel(scale, back, out):
    slots, width = back.shape
    npred, channels = out.shape[1:]
    turned = dot_dims(back[:, width - LANES :], identity(slots, channels), TN)
    at = lambda k: turned[8 + k * npred : 8 + (k + 1) * npred]
    lower, upper = (at(0) + at(1)) * scale, (at(2) + at(3)) * scale
    lanes = place((npred, channels - LANES), 1)
    second = jnp.where(lanes < slots - LANES, lower[:, LANES:], upper[:, : channels - LANES])
    for peer in range(out.shape[0]):
        out[peer, :, :LANES] = lower[:, :LANES]
        out[peer, :, LANES:] = second


def radiance_kernel(back, w_in, b_in, w_mid, b_mid, w_out, b_out, radiance):
    _, h2 = forward(back[:, : w_in.shape[0]], w_in, b_in, w_mid, b_mid)
    radiance[...] = (dot(h2, w_out[...]) + b_out[...]).astype(BF16)


def sum_kernel(shared, out):
    total = shared[0]
    for peer in range(1, shared.shape[0]):
        total = total + shared[peer]
    out[...] = total


def call(kernel, out, *args, flops=0, touched=0, space=pltpu.VMEM, scratch=(), grant=GRANT):
    return pl.pallas_call(
        kernel,
        out_shape=out,
        in_specs=[pl.BlockSpec(memory_space=space)] * len(args),
        out_specs=jax.tree.map(lambda _: pl.BlockSpec(memory_space=pltpu.VMEM), out),
        scratch_shapes=scratch,
        compiler_params=pltpu.CompilerParams(vmem_limit_bytes=grant),
        cost_estimate=pl.CostEstimate(flops=flops, bytes_accessed=touched, transcendentals=0),
    )(*args)


def on_device(
    state, departures, stencil, bilinear, counts, predictors, w_in, b_in, w_mid, b_mid, w_out, b_out
):
    slots, channels = departures.shape
    columns, feat = state.shape
    npred = predictors.shape[0]
    peers, rows = lax.axis_size("tx"), lax.axis_size("ty")
    cap = slots // peers
    scale = 1.0 / math.sqrt(slots * peers * rows)
    b_in, b_mid, b_out = b_in[None], b_mid[None], b_out[None]
    shape = jax.ShapeDtypeStruct

    inputs = (departures, stencil.T, bilinear.T, counts[None], predictors)
    packed = call(
        pack_kernel,
        shape((peers, cap, channels + LANES), BF16),
        *inputs,
        flops=40_000_000,
        touched=300_000,
        space=pl.ANY,
        scratch=[pltpu.VMEM(a.shape, a.dtype) for a in inputs]
        + [pltpu.SemaphoreType.DMA((len(inputs),))],
        grant=PACK_GRANT,
    )
    state = call(
        keep_kernel, shape(state.shape, BF16), state, flops=2_000_000_000, touched=2_000_000
    )
    got = exchange(packed, "tx").reshape(slots, -1)
    reply, profile = call(
        functools.partial(reply_kernel, npred),
        (shape((peers, cap, feat + LANES), BF16), shape((slots, feat), BF16)),
        got,
        state,
        flops=50_000_000,
        touched=500_000,
    )
    back = exchange(reply, "tx").reshape(slots, -1)
    state_grad, b_out = call(
        grad_kernel,
        (shape((columns, feat), F32), shape((1, channels), F32)),
        got,
        profile,
        w_in,
        b_in,
        w_mid,
        b_mid,
        w_out,
        b_out,
        flops=400_000_000,
        touched=2_000_000,
    )
    shared = call(
        functools.partial(bias_kernel, scale),
        shape((rows, npred, channels), F32),
        back,
        flops=10_000_000,
        touched=200_000,
    )
    shared = exchange(shared, "ty")
    radiance = call(
        radiance_kernel,
        shape((slots, channels), BF16),
        back,
        w_in,
        b_in,
        w_mid,
        b_mid,
        w_out,
        b_out,
        flops=2_000_000_000,
        touched=2_000_000,
    )
    bias_grad = call(
        sum_kernel, shape((npred, channels), F32), shared, flops=20_000, touched=70_000
    )
    return (radiance, state_grad, bias_grad)


def solution(mesh):
    both = P(("tx", "ty"), None)
    placed = (both, both, both, both, P(("tx", "ty")), P(None, ("tx", "ty"))) + (P(),) * 6
    return jax.shard_map(
        on_device,
        mesh=mesh,
        in_specs=placed,
        out_specs=(both, both, P()),
        check_vma=False,
    )
```

```python
import functools
import math

import jax
import jax.numpy as jnp
from jax import lax
from jax.experimental import pallas as pl
from jax.experimental.pallas import tpu as pltpu
from jax.sharding import PartitionSpec as P

F32, BF16, I32 = jnp.float32, jnp.bfloat16, jnp.int32
NT = (((1,), (1,)), ((), ()))
TN = (((0,), (0,)), ((), ()))
TILE_W = 32
LANES = 128
GRANT = 40 * 1024 * 1024
PACK_GRANT = 60 * 1024 * 1024


def exchange(block, axis):
    return lax.all_to_all(block, axis, split_axis=0, concat_axis=0, tiled=True)


def dot(a, b):
    return jnp.dot(a, b, preferred_element_type=F32)


def dot_dims(a, b, dims):
    return lax.dot_general(a, b, dims, preferred_element_type=F32)


def place(shape, dim):
    return lax.broadcasted_iota(I32, shape, dim)


def identity(rows, columns):
    shape = (rows, columns)
    return (place(shape, 0) == place(shape, 1)).astype(F32).astype(BF16)


def rounded(x):
    return x.astype(BF16).astype(F32)


def masked_by(departures, counts):
    slots, peers = departures.shape[0], counts.shape[1]
    cap = slots // peers
    holds = (place((slots, peers), 0) // cap == place((slots, peers), 1)).astype(F32).astype(BF16)
    counted = jnp.broadcast_to(counts[...].astype(F32), (8, peers)).astype(BF16)
    count_of = dot_dims(holds, counted, NT)[:, 0:1]
    live = (place((slots, 1), 0) % cap).astype(F32) < count_of
    return jnp.where(live, departures[...].astype(F32), 0.0).astype(BF16)


def keep_kernel(state, departures, counts, state_kept, dy):
    state_kept[...] = state[...]
    dy[...] = masked_by(departures, counts)


def pack_kernel(
    departures_hbm, stencil_hbm, bilinear_hbm, counts_hbm, predictors_hbm, out,
    departures, stencil, bilinear, counts, predictors, arrived
):
    pairs = (
        (counts_hbm, counts),
        (departures_hbm, departures),
        (predictors_hbm, predictors),
        (stencil_hbm, stencil),
        (bilinear_hbm, bilinear),
    )
    copies = [
        pltpu.make_async_copy(source, target, arrived.at[k])
        for k, (source, target) in enumerate(pairs)
    ]
    for copy in copies:
        copy.start()
    slots, channels = departures.shape
    peers = counts.shape[1]
    cap = slots // peers
    npred = predictors.shape[0]
    turn = identity(slots, slots)
    for copy in copies:
        copy.wait()
    dy = masked_by(departures, counts)

    pred = predictors[...]
    part0 = rounded(pred)
    part1 = rounded(pred - part0)
    part2 = pred - part0 - part1
    thirds = dot(jnp.concatenate([part0, part1, part2], axis=0).astype(BF16), dy)
    partial = thirds[:npred] + thirds[npred : 2 * npred] + thirds[2 * npred :]
    slot = place((slots, npred), 0) % (2 * cap) * 2
    which = place((slots, npred), 1)
    partial = partial.astype(BF16)
    for k in range(2):
        chosen = (which == slot + k).astype(F32).astype(BF16)
        out[:, :, LANES + k * channels : LANES + (k + 1) * channels] = (
            dot(chosen, partial).astype(BF16).reshape(peers, cap, channels)
        )

    corner = stencil[0:1, :]
    column = jnp.bitwise_and(corner, TILE_W - 1)
    row = (corner - column) // TILE_W
    rows = [bilinear[...].astype(F32), row.astype(F32), column.astype(F32)]
    rows.append(jnp.zeros((LANES - 6, slots), F32))
    extra = jnp.concatenate(rows, axis=0).astype(BF16)
    out[:, :, :LANES] = dot_dims(turn, extra, NT).astype(BF16).reshape(peers, cap, LANES)


def spread_of(extra, columns):
    extra = extra.astype(F32)
    corner = (extra[:, 4:5] * TILE_W + extra[:, 5:6]).astype(I32)
    delta = place((extra.shape[0], columns), 1) - corner
    spread = jnp.zeros(delta.shape, F32)
    for k, offset in enumerate((0, 1, TILE_W, TILE_W + 1)):
        spread = jnp.where(delta == offset, extra[:, k : k + 1], spread)
    return spread.astype(BF16)


def reply_kernel(cap, got, dy, state, out, terms, kept):
    slots = got.shape[0]
    feat = state.shape[1]
    mine = (place((8, slots), 1) % cap == place((8, slots), 0)).astype(F32).astype(BF16)
    terms[...] = dot(mine, got[:, LANES:])
    spread = spread_of(got[:, :LANES], state.shape[0])
    shape = out.shape[:2]
    profile = dot(spread, state[...]).astype(BF16)
    kept[...] = profile
    out[:, :, :feat] = profile.reshape(*shape, feat)
    out[:, :, feat:] = dy[...].reshape(*shape, dy.shape[1])


def forward(profile, w_in, b_in, w_mid, b_mid):
    h1 = jnp.tanh(dot(profile, w_in[...]) + b_in[...]).astype(BF16)
    h2 = jnp.tanh(dot(h1, w_mid[...]) + b_mid[...]).astype(BF16)
    return h1, h2


def hidden_kernel(
    got, profile, w_in, b_in, w_mid, b_mid, w_out, b_out, slope1, slope2, spread, b_kept
):
    slots = got.shape[0]
    b_kept[...] = b_out[...]
    h1, h2 = forward(profile[...], w_in, b_in, w_mid, b_mid)
    h1, h2 = h1.astype(F32), h2.astype(F32)
    slope1[...] = 1.0 - h1 * h1
    slope2[...] = 1.0 - h2 * h2
    extra = dot_dims(got[:, :LANES], identity(slots, slots), TN)
    corner = (extra[4:5] * TILE_W + extra[5:6]).astype(I32)
    delta = place(spread.shape, 0) - corner
    turned = jnp.zeros(spread.shape, F32)
    for k, offset in enumerate((0, 1, TILE_W, TILE_W + 1)):
        turned = jnp.where(delta == offset, extra[k : k + 1], turned)
    spread[...] = turned.astype(BF16)


def final_kernel(
    scale, back, spread, slope1, slope2, even, odd, w_in, b_in, w_mid, b_mid, w_out, b_out,
    state_grad, radiance, bias_grad, grad, sent
):
    feat = w_in.shape[0]
    channels = bias_grad.shape[1]
    g2 = dot_dims(back[:, feat:], w_out[...], NT)
    g2 = (g2 * slope2[...]).astype(BF16)
    g1 = dot_dims(g2, w_mid[...], NT)
    g1 = (g1 * slope1[...]).astype(BF16)
    dprofile = dot_dims(g1, w_in[...], NT).astype(BF16)
    grad[...] = dot(spread[...], dprofile)
    copy = pltpu.make_async_copy(grad, state_grad, sent)
    copy.start()

    _, last = forward(back[:, :feat], w_in, b_in, w_mid, b_mid)
    radiance[...] = (dot(last, w_out[...]) + b_out[...]).astype(BF16)

    for k, half in enumerate((even, odd)):
        for j in range(2):
            for e in range(2):
                row = 4 * k + 2 * j + e
                bias_grad[row : row + 1, :] = (
                    half[j : j + 1, e * channels : (e + 1) * channels] * scale
                )
    copy.wait()


def call(
    kernel, out, *args, flops=0, touched=0, space=pltpu.VMEM, scratch=(), grant=GRANT, places=None
):
    return pl.pallas_call(
        kernel,
        out_shape=out,
        in_specs=[pl.BlockSpec(memory_space=space)] * len(args),
        out_specs=places or jax.tree.map(lambda _: pl.BlockSpec(memory_space=pltpu.VMEM), out),
        scratch_shapes=scratch,
        compiler_params=pltpu.CompilerParams(vmem_limit_bytes=grant),
        cost_estimate=pl.CostEstimate(flops=flops, bytes_accessed=touched, transcendentals=0),
    )(*args)


def on_device(
    state, departures, stencil, bilinear, counts, predictors, w_in, b_in, w_mid, b_mid, w_out, b_out
):
    slots, channels = departures.shape
    columns, feat = state.shape
    npred = predictors.shape[0]
    peers, rows = lax.axis_size("tx"), lax.axis_size("ty")
    cap = slots // peers
    scale = 1.0 / math.sqrt(slots * peers * rows)
    b_in, b_mid, b_out = b_in[None], b_mid[None], b_out[None]
    shape = jax.ShapeDtypeStruct

    inputs = (departures, stencil.T, bilinear.T, counts[None], predictors)
    packed = call(
        pack_kernel,
        shape((peers, cap, LANES + 2 * channels), BF16),
        *inputs,
        flops=40_000_000,
        touched=300_000,
        space=pl.ANY,
        scratch=[pltpu.VMEM(a.shape, a.dtype) for a in inputs]
        + [pltpu.SemaphoreType.DMA((len(inputs),))],
        grant=PACK_GRANT,
    )
    state, dy = call(
        keep_kernel,
        (shape(state.shape, BF16), shape(departures.shape, BF16)),
        state,
        departures,
        counts[None],
        flops=2_000_000_000,
        touched=2_000_000,
    )
    got = exchange(packed, "tx").reshape(slots, -1)
    reply, terms, profile = call(
        functools.partial(reply_kernel, cap),
        (
            shape((peers, cap, feat + channels), BF16),
            shape((8, 2 * channels), F32),
            shape((slots, feat), BF16),
        ),
        got,
        dy,
        state,
        flops=50_000_000,
        touched=500_000,
    )
    back = exchange(reply, "tx").reshape(slots, -1)
    hid = w_in.shape[1]
    slope1, slope2, spread, b_out = call(
        hidden_kernel,
        (
            shape((slots, hid), F32),
            shape((slots, hid), F32),
            shape((columns, slots), BF16),
            shape((1, channels), F32),
        ),
        got,
        profile,
        w_in,
        b_in,
        w_mid,
        b_mid,
        w_out,
        b_out,
        flops=130_000_000,
        touched=1_000_000,
    )
    terms = lax.all_gather(terms, "ty").sum(axis=0)[:cap]
    other = lax.ppermute(terms, "tx", [(a, a ^ 1) for a in range(peers)])
    is_even = lax.axis_index("tx") % 2 == 0
    even = jnp.where(is_even, terms, other)
    odd = jnp.where(is_even, other, terms)
    state_grad, radiance, bias_grad = call(
        functools.partial(final_kernel, scale),
        (
            shape((columns, feat), F32),
            shape((slots, channels), BF16),
            shape((npred, channels), F32),
        ),
        back,
        spread,
        slope1,
        slope2,
        even,
        odd,
        w_in,
        b_in,
        w_mid,
        b_mid,
        w_out,
        b_out,
        flops=400_000_000,
        touched=2_000_000,
        scratch=[pltpu.VMEM((columns, feat), F32), pltpu.SemaphoreType.DMA],
        places=(
            pl.BlockSpec(memory_space=pl.ANY),
            pl.BlockSpec(memory_space=pltpu.VMEM),
            pl.BlockSpec(memory_space=pltpu.VMEM),
        ),
    )
    return (radiance, state_grad, bias_grad)


def solution(mesh):
    both = P(("tx", "ty"), None)
    placed = (both, both, both, both, P(("tx", "ty")), P(None, ("tx", "ty"))) + (P(),) * 6
    return jax.shard_map(
        on_device,
        mesh=mesh,
        in_specs=placed,
        out_specs=(both, both, P()),
        check_vma=False,
    )
```

```python
import functools
import math

import jax
import jax.numpy as jnp
from jax import lax
from jax.experimental import pallas as pl
from jax.experimental.pallas import tpu as pltpu
from jax.sharding import PartitionSpec as P

F32, BF16, I32 = jnp.float32, jnp.bfloat16, jnp.int32
NT = (((1,), (1,)), ((), ()))
TN = (((0,), (0,)), ((), ()))
TILE_W = 32
LANES = 128
GRANT = 40 * 1024 * 1024
PACK_GRANT = 60 * 1024 * 1024


def exchange(block, axis):
    return lax.all_to_all(block, axis, split_axis=0, concat_axis=0, tiled=True)


def dot(a, b):
    return jnp.dot(a, b, preferred_element_type=F32)


def dot_dims(a, b, dims):
    return lax.dot_general(a, b, dims, preferred_element_type=F32)


def place(shape, dim):
    return lax.broadcasted_iota(I32, shape, dim)


def identity(rows, columns):
    shape = (rows, columns)
    return (place(shape, 0) == place(shape, 1)).astype(F32).astype(BF16)


def rounded(x):
    return x.astype(BF16).astype(F32)


def masked_by(departures, counts):
    slots, peers = departures.shape[0], counts.shape[1]
    cap = slots // peers
    holds = (place((slots, peers), 0) // cap == place((slots, peers), 1)).astype(F32).astype(BF16)
    counted = jnp.broadcast_to(counts[...].astype(F32), (8, peers)).astype(BF16)
    count_of = dot_dims(holds, counted, NT)[:, 0:1]
    live = (place((slots, 1), 0) % cap).astype(F32) < count_of
    return jnp.where(live, departures[...].astype(F32), 0.0).astype(BF16)


def keep_kernel(state, departures, counts, b_in, b_mid, b_out, state_kept, dy, in_kept, mid_kept, out_kept):
    state_kept[...] = state[...]
    in_kept[...] = b_in[...]
    mid_kept[...] = b_mid[...]
    out_kept[...] = b_out[...]
    dy[...] = masked_by(departures, counts)


def pack_kernel(
    departures_hbm, stencil_hbm, bilinear_hbm, counts_hbm, predictors_hbm, out,
    departures, stencil, bilinear, counts, predictors, arrived
):
    pairs = (
        (counts_hbm, counts),
        (departures_hbm, departures),
        (predictors_hbm, predictors),
        (stencil_hbm, stencil),
        (bilinear_hbm, bilinear),
    )
    copies = [
        pltpu.make_async_copy(source, target, arrived.at[k])
        for k, (source, target) in enumerate(pairs)
    ]
    for copy in copies:
        copy.start()
    slots, channels = departures.shape
    peers = counts.shape[1]
    cap = slots // peers
    npred = predictors.shape[0]
    turn = identity(slots, slots)
    for copy in copies:
        copy.wait()
    dy = masked_by(departures, counts)

    pred = predictors[...]
    part0 = rounded(pred)
    part1 = rounded(pred - part0)
    part2 = pred - part0 - part1
    thirds = dot(jnp.concatenate([part0, part1, part2], axis=0).astype(BF16), dy)
    partial = thirds[:npred] + thirds[npred : 2 * npred] + thirds[2 * npred :]
    slot = place((slots, npred), 0) % (2 * cap) * 2
    which = place((slots, npred), 1)
    partial = partial.astype(BF16)
    for k in range(2):
        chosen = (which == slot + k).astype(F32).astype(BF16)
        out[:, :, LANES + k * channels : LANES + (k + 1) * channels] = (
            dot(chosen, partial).astype(BF16).reshape(peers, cap, channels)
        )

    corner = stencil[0:1, :]
    column = jnp.bitwise_and(corner, TILE_W - 1)
    row = (corner - column) // TILE_W
    rows = [bilinear[...].astype(F32), row.astype(F32), column.astype(F32)]
    rows.append(jnp.zeros((LANES - 6, slots), F32))
    extra = jnp.concatenate(rows, axis=0).astype(BF16)
    out[:, :, :LANES] = dot_dims(turn, extra, NT).astype(BF16).reshape(peers, cap, LANES)


def spread_of(extra, columns):
    extra = extra.astype(F32)
    corner = (extra[:, 4:5] * TILE_W + extra[:, 5:6]).astype(I32)
    delta = place((extra.shape[0], columns), 1) - corner
    spread = jnp.zeros(delta.shape, F32)
    for k, offset in enumerate((0, 1, TILE_W, TILE_W + 1)):
        spread = jnp.where(delta == offset, extra[:, k : k + 1], spread)
    return spread.astype(BF16)


def reply_kernel(cap, got, dy, state, out, terms, kept):
    slots = got.shape[0]
    feat = state.shape[1]
    mine = (place((8, slots), 1) % cap == place((8, slots), 0)).astype(F32).astype(BF16)
    terms[...] = dot(mine, got[:, LANES:])
    spread = spread_of(got[:, :LANES], state.shape[0])
    shape = out.shape[:2]
    profile = dot(spread, state[...]).astype(BF16)
    kept[...] = profile
    out[:, :, :feat] = profile.reshape(*shape, feat)
    out[:, :, feat:] = dy[...].reshape(*shape, dy.shape[1])


def forward(profile, w_in, b_in, w_mid, b_mid):
    h1 = jnp.tanh(dot(profile, w_in[...]) + b_in[...]).astype(BF16)
    h2 = jnp.tanh(dot(h1, w_mid[...]) + b_mid[...]).astype(BF16)
    return h1, h2


def hidden_kernel(profile, w_in, b_in, w_mid, b_mid, w_out, h1, h2):
    del w_out
    h1[...], h2[...] = forward(profile[...], w_in, b_in, w_mid, b_mid)


def final_kernel(
    scale, back, got, h1, h2, even, odd, w_in, b_in, w_mid, b_mid, w_out, b_out,
    state_grad, radiance, bias_grad
):
    feat = w_in.shape[0]
    channels = bias_grad.shape[1]
    h2f, h1f = h2[...].astype(F32), h1[...].astype(F32)
    g2 = dot_dims(back[:, feat:], w_out[...], NT)
    g2 = (g2 * (1.0 - h2f * h2f)).astype(BF16)
    g1 = dot_dims(g2, w_mid[...], NT)
    g1 = (g1 * (1.0 - h1f * h1f)).astype(BF16)
    dprofile = dot_dims(g1, w_in[...], NT).astype(BF16)
    spread = spread_of(got[:, :LANES], state_grad.shape[0])
    state_grad[...] = dot_dims(spread, dprofile, TN)

    _, last = forward(back[:, :feat], w_in, b_in, w_mid, b_mid)
    radiance[...] = (dot(last, w_out[...]) + b_out[...]).astype(BF16)

    for k, half in enumerate((even, odd)):
        for j in range(2):
            for e in range(2):
                row = 4 * k + 2 * j + e
                bias_grad[row : row + 1, :] = (
                    half[j : j + 1, e * channels : (e + 1) * channels] * scale
                )


def call(kernel, out, *args, flops=0, touched=0, space=pltpu.VMEM, scratch=(), grant=GRANT):
    return pl.pallas_call(
        kernel,
        out_shape=out,
        in_specs=[pl.BlockSpec(memory_space=space)] * len(args),
        out_specs=jax.tree.map(lambda _: pl.BlockSpec(memory_space=pltpu.VMEM), out),
        scratch_shapes=scratch,
        compiler_params=pltpu.CompilerParams(vmem_limit_bytes=grant),
        cost_estimate=pl.CostEstimate(flops=flops, bytes_accessed=touched, transcendentals=0),
    )(*args)


def on_device(
    state, departures, stencil, bilinear, counts, predictors, w_in, b_in, w_mid, b_mid, w_out, b_out
):
    slots, channels = departures.shape
    columns, feat = state.shape
    npred = predictors.shape[0]
    peers, rows = lax.axis_size("tx"), lax.axis_size("ty")
    cap = slots // peers
    scale = 1.0 / math.sqrt(slots * peers * rows)
    b_in, b_mid, b_out = b_in[None], b_mid[None], b_out[None]
    shape = jax.ShapeDtypeStruct

    inputs = (departures, stencil.T, bilinear.T, counts[None], predictors)
    packed = call(
        pack_kernel,
        shape((peers, cap, LANES + 2 * channels), BF16),
        *inputs,
        flops=40_000_000,
        touched=300_000,
        space=pl.ANY,
        scratch=[pltpu.VMEM(a.shape, a.dtype) for a in inputs]
        + [pltpu.SemaphoreType.DMA((len(inputs),))],
        grant=PACK_GRANT,
    )
    state, dy, b_in, b_mid, b_out = call(
        keep_kernel,
        (shape(state.shape, BF16), shape(departures.shape, BF16))
        + tuple(shape(b.shape, F32) for b in (b_in, b_mid, b_out)),
        state,
        departures,
        counts[None],
        b_in,
        b_mid,
        b_out,
        flops=2_000_000_000,
        touched=2_000_000,
    )
    got = exchange(packed, "tx").reshape(slots, -1)
    reply, terms, profile = call(
        functools.partial(reply_kernel, cap),
        (
            shape((peers, cap, feat + channels), BF16),
            shape((8, 2 * channels), F32),
            shape((slots, feat), BF16),
        ),
        got,
        dy,
        state,
        flops=50_000_000,
        touched=500_000,
    )
    back = exchange(reply, "tx").reshape(slots, -1)
    h1, h2 = call(
        hidden_kernel,
        (shape((slots, w_in.shape[1]), BF16),) * 2,
        profile,
        w_in,
        b_in,
        w_mid,
        b_mid,
        w_out,
        flops=130_000_000,
        touched=1_000_000,
    )
    terms = lax.psum(terms[:cap], "ty")
    other = lax.ppermute(terms, "tx", [(a, a ^ 1) for a in range(peers)])
    is_even = lax.axis_index("tx") % 2 == 0
    even = jnp.where(is_even, terms, other)
    odd = jnp.where(is_even, other, terms)
    state_grad, radiance, bias_grad = call(
        functools.partial(final_kernel, scale),
        (
            shape((columns, feat), F32),
            shape((slots, channels), BF16),
            shape((npred, channels), F32),
        ),
        back,
        got,
        h1,
        h2,
        even,
        odd,
        w_in,
        b_in,
        w_mid,
        b_mid,
        w_out,
        b_out,
        flops=400_000_000,
        touched=2_000_000,
    )
    return (radiance, state_grad, bias_grad)


def solution(mesh):
    both = P(("tx", "ty"), None)
    placed = (both, both, both, both, P(("tx", "ty")), P(None, ("tx", "ty"))) + (P(),) * 6
    return jax.shard_map(
        on_device,
        mesh=mesh,
        in_specs=placed,
        out_specs=(both, both, P()),
        check_vma=False,
    )
```

```python
import functools
import math

import jax
import jax.numpy as jnp
from jax import lax
from jax.experimental import pallas as pl
from jax.experimental.pallas import tpu as pltpu
from jax.sharding import PartitionSpec as P

F32, BF16, I32 = jnp.float32, jnp.bfloat16, jnp.int32
NT = (((1,), (1,)), ((), ()))
TN = (((0,), (0,)), ((), ()))
TILE_W = 32
LANES = 128
GRANT = 40 * 1024 * 1024
PACK_GRANT = 60 * 1024 * 1024


def exchange(block, axis):
    return lax.all_to_all(block, axis, split_axis=0, concat_axis=0, tiled=True)


def dot(a, b):
    return jnp.dot(a, b, preferred_element_type=F32)


def dot_dims(a, b, dims):
    return lax.dot_general(a, b, dims, preferred_element_type=F32)


def place(shape, dim):
    return lax.broadcasted_iota(I32, shape, dim)


def identity(rows, columns):
    shape = (rows, columns)
    return (place(shape, 0) == place(shape, 1)).astype(F32).astype(BF16)


def rounded(x):
    return x.astype(BF16).astype(F32)


def masked_by(departures, counts):
    slots, peers = departures.shape[0], counts.shape[1]
    cap = slots // peers
    holds = (place((slots, peers), 0) // cap == place((slots, peers), 1)).astype(F32).astype(BF16)
    counted = jnp.broadcast_to(counts[...].astype(F32), (8, peers)).astype(BF16)
    count_of = dot_dims(holds, counted, NT)[:, 0:1]
    live = (place((slots, 1), 0) % cap).astype(F32) < count_of
    return jnp.where(live, departures[...].astype(F32), 0.0).astype(BF16)


def keep_kernel(state, departures, counts, b_in, b_mid, b_out, state_kept, dy, in_kept, mid_kept, out_kept):
    state_kept[...] = state[...]
    in_kept[...] = b_in[...]
    mid_kept[...] = b_mid[...]
    out_kept[...] = b_out[...]
    dy[...] = masked_by(departures, counts)


def pack_kernel(
    departures_hbm, stencil_hbm, bilinear_hbm, counts_hbm, predictors_hbm, out,
    departures, stencil, bilinear, counts, predictors, arrived
):
    pairs = (
        (counts_hbm, counts),
        (departures_hbm, departures),
        (predictors_hbm, predictors),
        (stencil_hbm, stencil),
        (bilinear_hbm, bilinear),
    )
    copies = [
        pltpu.make_async_copy(source, target, arrived.at[k])
        for k, (source, target) in enumerate(pairs)
    ]
    for copy in copies:
        copy.start()
    slots, channels = departures.shape
    peers = counts.shape[1]
    cap = slots // peers
    npred = predictors.shape[0]
    turn = identity(slots, slots)
    for copy in copies:
        copy.wait()
    dy = masked_by(departures, counts)

    pred = predictors[...]
    part0 = rounded(pred)
    part1 = rounded(pred - part0)
    part2 = pred - part0 - part1
    thirds = dot(jnp.concatenate([part0, part1, part2], axis=0).astype(BF16), dy)
    partial = thirds[:npred] + thirds[npred : 2 * npred] + thirds[2 * npred :]
    slot = place((slots, npred), 0) % (2 * cap) * 2
    which = place((slots, npred), 1)
    partial = partial.astype(BF16)
    for k in range(2):
        chosen = (which == slot + k).astype(F32).astype(BF16)
        out[:, :, LANES + k * channels : LANES + (k + 1) * channels] = (
            dot(chosen, partial).astype(BF16).reshape(peers, cap, channels)
        )

    corner = stencil[0:1, :]
    column = jnp.bitwise_and(corner, TILE_W - 1)
    row = (corner - column) // TILE_W
    rows = [bilinear[...].astype(F32), row.astype(F32), column.astype(F32)]
    rows.append(jnp.zeros((LANES - 6, slots), F32))
    extra = jnp.concatenate(rows, axis=0).astype(BF16)
    out[:, :, :LANES] = dot_dims(turn, extra, NT).astype(BF16).reshape(peers, cap, LANES)


def spread_of(extra, columns):
    extra = extra.astype(F32)
    corner = (extra[:, 4:5] * TILE_W + extra[:, 5:6]).astype(I32)
    delta = place((extra.shape[0], columns), 1) - corner
    spread = jnp.zeros(delta.shape, F32)
    for k, offset in enumerate((0, 1, TILE_W, TILE_W + 1)):
        spread = jnp.where(delta == offset, extra[:, k : k + 1], spread)
    return spread.astype(BF16)


def reply_kernel(cap, got, dy, state, out, terms, kept):
    slots = got.shape[0]
    feat = state.shape[1]
    mine = (place((8, slots), 1) % cap == place((8, slots), 0)).astype(F32).astype(BF16)
    terms[...] = dot(mine, got[:, LANES:])
    spread = spread_of(got[:, :LANES], state.shape[0])
    shape = out.shape[:2]
    profile = dot(spread, state[...]).astype(BF16)
    kept[...] = profile
    out[:, :, :feat] = profile.reshape(*shape, feat)
    out[:, :, feat:] = dy[...].reshape(*shape, dy.shape[1])


def forward(profile, w_in, b_in, w_mid, b_mid):
    h1 = jnp.tanh(dot(profile, w_in[...]) + b_in[...]).astype(BF16)
    h2 = jnp.tanh(dot(h1, w_mid[...]) + b_mid[...]).astype(BF16)
    return h1, h2


def hidden_kernel(profile, w_in, b_in, w_mid, b_mid, w_out, h1, h2):
    del w_out
    h1[...], h2[...] = forward(profile[...], w_in, b_in, w_mid, b_mid)


def final_kernel(
    back, got, h1, h2, w_in, b_in, w_mid, b_mid, w_out, b_out, state_grad, radiance, one
):
    feat = w_in.shape[0]
    h2f, h1f = h2[...].astype(F32), h1[...].astype(F32)
    g2 = dot_dims(back[:, feat:], w_out[...], NT)
    g2 = (g2 * (1.0 - h2f * h2f)).astype(BF16)
    g1 = dot_dims(g2, w_mid[...], NT)
    g1 = (g1 * (1.0 - h1f * h1f)).astype(BF16)
    dprofile = dot_dims(g1, w_in[...], NT).astype(BF16)
    spread = spread_of(got[:, :LANES], state_grad.shape[0])
    state_grad[...] = dot_dims(spread, dprofile, TN)

    _, last = forward(back[:, :feat], w_in, b_in, w_mid, b_mid)
    radiance[...] = (dot(last, w_out[...]) + b_out[...]).astype(BF16)
    one[...] = jnp.ones(one.shape, F32)


def bias_kernel(scale, one, even, odd, bias_grad):
    channels = bias_grad.shape[1]
    scale = one[0:1, 0:1] * scale
    for k, half in enumerate((even, odd)):
        for j in range(2):
            for e in range(2):
                row = 4 * k + 2 * j + e
                bias_grad[row : row + 1, :] = (
                    half[j : j + 1, e * channels : (e + 1) * channels] * scale
                )


def call(kernel, out, *args, flops=0, touched=0, space=pltpu.VMEM, scratch=(), grant=GRANT):
    return pl.pallas_call(
        kernel,
        out_shape=out,
        in_specs=[pl.BlockSpec(memory_space=space)] * len(args),
        out_specs=jax.tree.map(lambda _: pl.BlockSpec(memory_space=pltpu.VMEM), out),
        scratch_shapes=scratch,
        compiler_params=pltpu.CompilerParams(vmem_limit_bytes=grant),
        cost_estimate=pl.CostEstimate(flops=flops, bytes_accessed=touched, transcendentals=0),
    )(*args)


def on_device(
    state, departures, stencil, bilinear, counts, predictors, w_in, b_in, w_mid, b_mid, w_out, b_out
):
    slots, channels = departures.shape
    columns, feat = state.shape
    npred = predictors.shape[0]
    peers, rows = lax.axis_size("tx"), lax.axis_size("ty")
    cap = slots // peers
    scale = 1.0 / math.sqrt(slots * peers * rows)
    b_in, b_mid, b_out = b_in[None], b_mid[None], b_out[None]
    shape = jax.ShapeDtypeStruct

    inputs = (departures, stencil.T, bilinear.T, counts[None], predictors)
    packed = call(
        pack_kernel,
        shape((peers, cap, LANES + 2 * channels), BF16),
        *inputs,
        flops=40_000_000,
        touched=300_000,
        space=pl.ANY,
        scratch=[pltpu.VMEM(a.shape, a.dtype) for a in inputs]
        + [pltpu.SemaphoreType.DMA((len(inputs),))],
        grant=PACK_GRANT,
    )
    state, dy, b_in, b_mid, b_out = call(
        keep_kernel,
        (shape(state.shape, BF16), shape(departures.shape, BF16))
        + tuple(shape(b.shape, F32) for b in (b_in, b_mid, b_out)),
        state,
        departures,
        counts[None],
        b_in,
        b_mid,
        b_out,
        flops=2_000_000_000,
        touched=2_000_000,
    )
    got = exchange(packed, "tx").reshape(slots, -1)
    reply, terms, profile = call(
        functools.partial(reply_kernel, cap),
        (
            shape((peers, cap, feat + channels), BF16),
            shape((8, 2 * channels), F32),
            shape((slots, feat), BF16),
        ),
        got,
        dy,
        state,
        flops=50_000_000,
        touched=500_000,
    )
    back = exchange(reply, "tx").reshape(slots, -1)
    h1, h2 = call(
        hidden_kernel,
        (shape((slots, w_in.shape[1]), BF16),) * 2,
        profile,
        w_in,
        b_in,
        w_mid,
        b_mid,
        w_out,
        flops=130_000_000,
        touched=1_000_000,
    )
    terms = lax.psum(terms[:cap], "ty")
    terms, back = lax.optimization_barrier((terms, back))
    other = lax.ppermute(terms, "tx", [(a, a ^ 1) for a in range(peers)])
    is_even = lax.axis_index("tx") % 2 == 0
    even = jnp.where(is_even, terms, other)
    odd = jnp.where(is_even, other, terms)
    state_grad, radiance, one = call(
        final_kernel,
        (shape((columns, feat), F32), shape((slots, channels), BF16), shape((8, LANES), F32)),
        back,
        got,
        h1,
        h2,
        w_in,
        b_in,
        w_mid,
        b_mid,
        w_out,
        b_out,
        flops=3_000_000_000,
        touched=2_000_000,
    )
    bias_grad = call(
        functools.partial(bias_kernel, scale),
        shape((npred, channels), F32),
        one,
        even,
        odd,
        flops=2_000,
        touched=20_000,
    )
    return (radiance, state_grad, bias_grad)


def solution(mesh):
    both = P(("tx", "ty"), None)
    placed = (both, both, both, both, P(("tx", "ty")), P(None, ("tx", "ty"))) + (P(),) * 6
    return jax.shard_map(
        on_device,
        mesh=mesh,
        in_specs=placed,
        out_specs=(both, both, P()),
        check_vma=False,
    )
```

```python
import functools
import math

import jax
import jax.numpy as jnp
from jax import lax
from jax.experimental import pallas as pl
from jax.experimental.pallas import tpu as pltpu
from jax.sharding import PartitionSpec as P

F32, BF16, I32 = jnp.float32, jnp.bfloat16, jnp.int32
NT = (((1,), (1,)), ((), ()))
TN = (((0,), (0,)), ((), ()))
TILE_W = 32
LANES = 128
GRANT = 40 * 1024 * 1024
PACK_GRANT = 60 * 1024 * 1024


def exchange(block, axis):
    return lax.all_to_all(block, axis, split_axis=0, concat_axis=0, tiled=True)


def dot(a, b):
    return jnp.dot(a, b, preferred_element_type=F32)


def dot_dims(a, b, dims):
    return lax.dot_general(a, b, dims, preferred_element_type=F32)


def place(shape, dim):
    return lax.broadcasted_iota(I32, shape, dim)


def identity(rows, columns):
    shape = (rows, columns)
    return (place(shape, 0) == place(shape, 1)).astype(F32).astype(BF16)


def rounded(x):
    return x.astype(BF16).astype(F32)


def masked_by(departures, counts):
    slots, peers = departures.shape[0], counts.shape[1]
    cap = slots // peers
    holds = (place((slots, peers), 0) // cap == place((slots, peers), 1)).astype(F32).astype(BF16)
    counted = jnp.broadcast_to(counts[...].astype(F32), (8, peers)).astype(BF16)
    count_of = dot_dims(holds, counted, NT)[:, 0:1]
    live = (place((slots, 1), 0) % cap).astype(F32) < count_of
    return jnp.where(live, departures[...].astype(F32), 0.0).astype(BF16)


def keep_kernel(state, departures, counts, b_in, b_mid, b_out, state_kept, dy, in_kept, mid_kept, out_kept):
    state_kept[...] = state[...]
    in_kept[...] = b_in[...]
    mid_kept[...] = b_mid[...]
    out_kept[...] = b_out[...]
    dy[...] = masked_by(departures, counts)


def partial_kernel(
    departures_hbm, counts_hbm, predictors_hbm, stencil_hbm, bilinear_hbm, own, other, meta,
    departures, counts, predictors, stencil, bilinear, arrived
):
    pairs = (
        (counts_hbm, counts),
        (departures_hbm, departures),
        (predictors_hbm, predictors),
        (stencil_hbm, stencil),
        (bilinear_hbm, bilinear),
    )
    copies = [
        pltpu.make_async_copy(source, target, arrived.at[k])
        for k, (source, target) in enumerate(pairs)
    ]
    for copy in copies:
        copy.start()
    for copy in copies:
        copy.wait()
    npred = predictors.shape[0]
    dy = masked_by(departures, counts)
    pred = predictors[...]
    part0 = rounded(pred)
    part1 = rounded(pred - part0)
    part2 = pred - part0 - part1
    thirds = dot(jnp.concatenate([part0, part1, part2], axis=0).astype(BF16), dy)
    partial = thirds[:npred] + thirds[npred : 2 * npred] + thirds[2 * npred :]
    half = npred // 2
    first = lax.axis_index("ty") % 2 == 0
    own[...] = jnp.where(first, partial[:half], partial[half:])
    other[...] = jnp.where(first, partial[half:], partial[:half])
    slots = departures.shape[0]
    corner = stencil[0:1, :]
    column = jnp.bitwise_and(corner, TILE_W - 1)
    row = (corner - column) // TILE_W
    rows = [bilinear[...].astype(F32), row.astype(F32), column.astype(F32)]
    rows.append(jnp.zeros((LANES - 6, slots), F32))
    extra = jnp.concatenate(rows, axis=0).astype(BF16)
    extra = dot_dims(identity(slots, slots), extra, NT).astype(BF16)
    meta[...] = extra


def pack_kernel(meta, own, given, out):
    peers, cap = out.shape[:2]
    slots = peers * cap
    half, channels = own.shape
    joined = own[...] + given[...]
    joined = jnp.concatenate([joined, jnp.zeros((8 - half, channels), F32)], axis=0).astype(BF16)
    slot = place((slots, 8), 0) % cap * 2
    which = place((slots, 8), 1)
    for k in range(2):
        chosen = (which == slot + k).astype(F32).astype(BF16)
        out[:, :, LANES + k * channels : LANES + (k + 1) * channels] = (
            dot(chosen, joined).astype(BF16).reshape(peers, cap, channels)
        )
    out[:, :, :LANES] = meta[...].reshape(peers, cap, LANES)


def spread_of(extra, columns):
    extra = extra.astype(F32)
    corner = (extra[:, 4:5] * TILE_W + extra[:, 5:6]).astype(I32)
    delta = place((extra.shape[0], columns), 1) - corner
    spread = jnp.zeros(delta.shape, F32)
    for k, offset in enumerate((0, 1, TILE_W, TILE_W + 1)):
        spread = jnp.where(delta == offset, extra[:, k : k + 1], spread)
    return spread.astype(BF16)


def reply_kernel(cap, got, dy, state, out, terms, kept):
    slots = got.shape[0]
    feat = state.shape[1]
    mine = (place((8, slots), 1) % cap == place((8, slots), 0)).astype(F32).astype(BF16)
    terms[...] = dot(mine, got[:, LANES:])
    spread = spread_of(got[:, :LANES], state.shape[0])
    shape = out.shape[:2]
    profile = dot(spread, state[...]).astype(BF16)
    kept[...] = profile
    out[:, :, :feat] = profile.reshape(*shape, feat)
    out[:, :, feat:] = dy[...].reshape(*shape, dy.shape[1])


def forward(profile, w_in, b_in, w_mid, b_mid):
    h1 = jnp.tanh(dot(profile, w_in[...]) + b_in[...]).astype(BF16)
    h2 = jnp.tanh(dot(h1, w_mid[...]) + b_mid[...]).astype(BF16)
    return h1, h2


def hidden_kernel(profile, w_in, b_in, w_mid, b_mid, w_out, h1, h2):
    del w_out
    h1[...], h2[...] = forward(profile[...], w_in, b_in, w_mid, b_mid)


def final_kernel(
    scale, back, got, h1, h2, terms, w_in, b_in, w_mid, b_mid, w_out, b_out,
    state_grad, radiance, bias_grad
):
    feat = w_in.shape[0]
    channels = bias_grad.shape[1]
    h2f, h1f = h2[...].astype(F32), h1[...].astype(F32)
    g2 = dot_dims(back[:, feat:], w_out[...], NT)
    g2 = (g2 * (1.0 - h2f * h2f)).astype(BF16)
    g1 = dot_dims(g2, w_mid[...], NT)
    g1 = (g1 * (1.0 - h1f * h1f)).astype(BF16)
    dprofile = dot_dims(g1, w_in[...], NT).astype(BF16)
    spread = spread_of(got[:, :LANES], state_grad.shape[0])
    state_grad[...] = dot_dims(spread, dprofile, TN)

    _, last = forward(back[:, :feat], w_in, b_in, w_mid, b_mid)
    radiance[...] = (dot(last, w_out[...]) + b_out[...]).astype(BF16)

    for j in range(terms.shape[0]):
        for e in range(2):
            row = 2 * j + e
            bias_grad[row : row + 1, :] = (
                terms[j : j + 1, e * channels : (e + 1) * channels] * scale
            )


def call(kernel, out, *args, flops=0, touched=0, space=pltpu.VMEM, scratch=(), grant=GRANT):
    return pl.pallas_call(
        kernel,
        out_shape=out,
        in_specs=[pl.BlockSpec(memory_space=space)] * len(args),
        out_specs=jax.tree.map(lambda _: pl.BlockSpec(memory_space=pltpu.VMEM), out),
        scratch_shapes=scratch,
        compiler_params=pltpu.CompilerParams(vmem_limit_bytes=grant),
        cost_estimate=pl.CostEstimate(flops=flops, bytes_accessed=touched, transcendentals=0),
    )(*args)


def on_device(
    state, departures, stencil, bilinear, counts, predictors, w_in, b_in, w_mid, b_mid, w_out, b_out
):
    slots, channels = departures.shape
    columns, feat = state.shape
    npred = predictors.shape[0]
    peers, rows = lax.axis_size("tx"), lax.axis_size("ty")
    cap = slots // peers
    scale = 1.0 / math.sqrt(slots * peers * rows)
    b_in, b_mid, b_out = b_in[None], b_mid[None], b_out[None]
    shape = jax.ShapeDtypeStruct

    inputs = (departures, counts[None], predictors, stencil.T, bilinear.T)
    own, other, meta = call(
        partial_kernel,
        (shape((npred // 2, channels), F32),) * 2 + (shape((slots, LANES), BF16),),
        *inputs,
        flops=20_000_000,
        touched=200_000,
        space=pl.ANY,
        scratch=[pltpu.VMEM(a.shape, a.dtype) for a in inputs]
        + [pltpu.SemaphoreType.DMA((len(inputs),))],
        grant=PACK_GRANT,
    )
    given = lax.ppermute(other, "ty", [(b, b ^ 1) for b in range(rows)])
    packed = call(
        pack_kernel,
        shape((peers, cap, LANES + 2 * channels), BF16),
        meta,
        own,
        given,
        flops=20_000_000,
        touched=300_000,
    )
    state, dy, b_in, b_mid, b_out = call(
        keep_kernel,
        (shape(state.shape, BF16), shape(departures.shape, BF16))
        + tuple(shape(b.shape, F32) for b in (b_in, b_mid, b_out)),
        state,
        departures,
        counts[None],
        b_in,
        b_mid,
        b_out,
        flops=2_000_000_000,
        touched=2_000_000,
    )
    got = exchange(packed, "tx").reshape(slots, -1)
    reply, terms, profile = call(
        functools.partial(reply_kernel, cap),
        (
            shape((peers, cap, feat + channels), BF16),
            shape((8, 2 * channels), F32),
            shape((slots, feat), BF16),
        ),
        got,
        dy,
        state,
        flops=50_000_000,
        touched=500_000,
    )
    back = exchange(reply, "tx").reshape(slots, -1)
    h1, h2 = call(
        hidden_kernel,
        (shape((slots, w_in.shape[1]), BF16),) * 2,
        profile,
        w_in,
        b_in,
        w_mid,
        b_mid,
        w_out,
        flops=130_000_000,
        touched=1_000_000,
    )
    terms = terms[:cap]
    first = lax.axis_index("ty") % 2 == 0
    even = jnp.where(first, terms, 0.0)
    odd = jnp.where(first, 0.0, terms)
    terms = lax.psum(jnp.concatenate([even, odd], axis=0), "ty")
    state_grad, radiance, bias_grad = call(
        functools.partial(final_kernel, scale),
        (
            shape((columns, feat), F32),
            shape((slots, channels), BF16),
            shape((npred, channels), F32),
        ),
        back,
        got,
        h1,
        h2,
        terms,
        w_in,
        b_in,
        w_mid,
        b_mid,
        w_out,
        b_out,
        flops=400_000_000,
        touched=2_000_000,
    )
    return (radiance, state_grad, bias_grad)


def solution(mesh):
    both = P(("tx", "ty"), None)
    placed = (both, both, both, both, P(("tx", "ty")), P(None, ("tx", "ty"))) + (P(),) * 6
    return jax.shard_map(
        on_device,
        mesh=mesh,
        in_specs=placed,
        out_specs=(both, both, P()),
        check_vma=False,
    )
```

```python
import functools
import math

import jax
import jax.numpy as jnp
from jax import lax
from jax.experimental import pallas as pl
from jax.experimental.pallas import tpu as pltpu
from jax.sharding import PartitionSpec as P

F32, BF16, I32 = jnp.float32, jnp.bfloat16, jnp.int32
NT = (((1,), (1,)), ((), ()))
TN = (((0,), (0,)), ((), ()))
TILE_W = 32
LANES = 128
GRANT = 40 * 1024 * 1024
PACK_GRANT = 60 * 1024 * 1024


def exchange(block, axis):
    return lax.all_to_all(block, axis, split_axis=0, concat_axis=0, tiled=True)


def dot(a, b):
    return jnp.dot(a, b, preferred_element_type=F32)


def dot_dims(a, b, dims):
    return lax.dot_general(a, b, dims, preferred_element_type=F32)


def place(shape, dim):
    return lax.broadcasted_iota(I32, shape, dim)


def identity(rows, columns):
    shape = (rows, columns)
    return (place(shape, 0) == place(shape, 1)).astype(F32).astype(BF16)


def rounded(x):
    return x.astype(BF16).astype(F32)


def masked_by(departures, counts):
    slots, peers = departures.shape[0], counts.shape[1]
    cap = slots // peers
    holds = (place((slots, peers), 0) // cap == place((slots, peers), 1)).astype(F32).astype(BF16)
    counted = jnp.broadcast_to(counts[...].astype(F32), (8, peers)).astype(BF16)
    count_of = dot_dims(holds, counted, NT)[:, 0:1]
    live = (place((slots, 1), 0) % cap).astype(F32) < count_of
    return jnp.where(live, departures[...].astype(F32), 0.0).astype(BF16)


def keep_kernel(state, departures, counts, b_in, b_mid, b_out, state_kept, dy, in_kept, mid_kept, out_kept):
    state_kept[...] = state[...]
    in_kept[...] = b_in[...]
    mid_kept[...] = b_mid[...]
    out_kept[...] = b_out[...]
    dy[...] = masked_by(departures, counts)


def pack_kernel(
    departures_hbm, stencil_hbm, bilinear_hbm, counts_hbm, predictors_hbm, out,
    departures, stencil, bilinear, counts, predictors, arrived
):
    pairs = (
        (counts_hbm, counts),
        (departures_hbm, departures),
        (predictors_hbm, predictors),
        (stencil_hbm, stencil),
        (bilinear_hbm, bilinear),
    )
    copies = [
        pltpu.make_async_copy(source, target, arrived.at[k])
        for k, (source, target) in enumerate(pairs)
    ]
    for copy in copies:
        copy.start()
    slots, channels = departures.shape
    peers = counts.shape[1]
    cap = slots // peers
    npred = predictors.shape[0]
    turn = identity(slots, slots)
    for copy in copies:
        copy.wait()
    dy = masked_by(departures, counts)

    pred = predictors[...]
    part0 = rounded(pred)
    part1 = rounded(pred - part0)
    part2 = pred - part0 - part1
    thirds = dot(jnp.concatenate([part0, part1, part2], axis=0).astype(BF16), dy)
    partial = thirds[:npred] + thirds[npred : 2 * npred] + thirds[2 * npred :]
    slot = place((slots, npred), 0) % (2 * cap) * 2
    which = place((slots, npred), 1)
    partial = partial.astype(BF16)
    for k in range(2):
        chosen = (which == slot + k).astype(F32).astype(BF16)
        out[:, :, LANES + k * channels : LANES + (k + 1) * channels] = (
            dot(chosen, partial).astype(BF16).reshape(peers, cap, channels)
        )

    corner = stencil[0:1, :]
    column = jnp.bitwise_and(corner, TILE_W - 1)
    row = (corner - column) // TILE_W
    rows = [bilinear[...].astype(F32), row.astype(F32), column.astype(F32)]
    rows.append(jnp.zeros((LANES - 6, slots), F32))
    extra = jnp.concatenate(rows, axis=0).astype(BF16)
    out[:, :, :LANES] = dot_dims(turn, extra, NT).astype(BF16).reshape(peers, cap, LANES)


def spread_of(extra, columns):
    extra = extra.astype(F32)
    corner = (extra[:, 4:5] * TILE_W + extra[:, 5:6]).astype(I32)
    delta = place((extra.shape[0], columns), 1) - corner
    spread = jnp.zeros(delta.shape, F32)
    for k, offset in enumerate((0, 1, TILE_W, TILE_W + 1)):
        spread = jnp.where(delta == offset, extra[:, k : k + 1], spread)
    return spread.astype(BF16)


def reply_kernel(cap, got, dy, state, out, terms, kept):
    slots = got.shape[0]
    feat = state.shape[1]
    mine = (place((8, slots), 1) % cap == place((8, slots), 0)).astype(F32).astype(BF16)
    terms[...] = dot(mine, got[:, LANES:])
    spread = spread_of(got[:, :LANES], state.shape[0])
    shape = out.shape[:2]
    profile = dot(spread, state[...]).astype(BF16)
    kept[...] = profile
    out[:, :, :feat] = profile.reshape(*shape, feat)
    out[:, :, feat:] = dy[...].reshape(*shape, dy.shape[1])


def forward(profile, w_in, b_in, w_mid, b_mid):
    h1 = jnp.tanh(dot(profile, w_in[...]) + b_in[...]).astype(BF16)
    h2 = jnp.tanh(dot(h1, w_mid[...]) + b_mid[...]).astype(BF16)
    return h1, h2


def hidden_kernel(profile, w_in, b_in, w_mid, b_mid, w_out, h1, h2):
    del w_out
    h1[...], h2[...] = forward(profile[...], w_in, b_in, w_mid, b_mid)


def final_kernel(
    scale, back, got, h1, h2, even, odd, w_in, b_in, w_mid, b_mid, w_out, b_out,
    state_grad, radiance, bias_grad
):
    feat = w_in.shape[0]
    channels = bias_grad.shape[1]
    h2f, h1f = h2[...].astype(F32), h1[...].astype(F32)
    g2 = dot_dims(back[:, feat:], w_out[...], NT)
    g2 = (g2 * (1.0 - h2f * h2f)).astype(BF16)
    g1 = dot_dims(g2, w_mid[...], NT)
    g1 = (g1 * (1.0 - h1f * h1f)).astype(BF16)
    dprofile = dot_dims(g1, w_in[...], NT).astype(BF16)
    spread = spread_of(got[:, :LANES], state_grad.shape[0])
    state_grad[...] = dot_dims(spread, dprofile, TN)

    _, last = forward(back[:, :feat], w_in, b_in, w_mid, b_mid)
    radiance[...] = (dot(last, w_out[...]) + b_out[...]).astype(BF16)

    for k, half in enumerate((even, odd)):
        for j in range(2):
            for e in range(2):
                row = 4 * k + 2 * j + e
                bias_grad[row : row + 1, :] = (
                    half[j : j + 1, e * channels : (e + 1) * channels] * scale
                )


def call(kernel, out, *args, flops=0, touched=0, space=pltpu.VMEM, scratch=(), grant=GRANT):
    return pl.pallas_call(
        kernel,
        out_shape=out,
        in_specs=[pl.BlockSpec(memory_space=space)] * len(args),
        out_specs=jax.tree.map(lambda _: pl.BlockSpec(memory_space=pltpu.VMEM), out),
        scratch_shapes=scratch,
        compiler_params=pltpu.CompilerParams(vmem_limit_bytes=grant),
        cost_estimate=pl.CostEstimate(flops=flops, bytes_accessed=touched, transcendentals=0),
    )(*args)


def on_device(
    state, departures, stencil, bilinear, counts, predictors, w_in, b_in, w_mid, b_mid, w_out, b_out
):
    slots, channels = departures.shape
    columns, feat = state.shape
    npred = predictors.shape[0]
    peers, rows = lax.axis_size("tx"), lax.axis_size("ty")
    cap = slots // peers
    scale = 1.0 / math.sqrt(slots * peers * rows)
    b_in, b_mid, b_out = b_in[None], b_mid[None], b_out[None]
    shape = jax.ShapeDtypeStruct

    inputs = (departures, stencil.T, bilinear.T, counts[None], predictors)
    packed = call(
        pack_kernel,
        shape((peers, cap, LANES + 2 * channels), BF16),
        *inputs,
        flops=40_000_000,
        touched=300_000,
        space=pl.ANY,
        scratch=[pltpu.VMEM(a.shape, a.dtype) for a in inputs]
        + [pltpu.SemaphoreType.DMA((len(inputs),))],
        grant=PACK_GRANT,
    )
    state, dy, b_in, b_mid, b_out = call(
        keep_kernel,
        (shape(state.shape, BF16), shape(departures.shape, BF16))
        + tuple(shape(b.shape, F32) for b in (b_in, b_mid, b_out)),
        state,
        departures,
        counts[None],
        b_in,
        b_mid,
        b_out,
        flops=2_000_000_000,
        touched=2_000_000,
    )
    got = exchange(packed, "tx").reshape(slots, -1)
    reply, terms, profile = call(
        functools.partial(reply_kernel, cap),
        (
            shape((peers, cap, feat + channels), BF16),
            shape((8, 2 * channels), F32),
            shape((slots, feat), BF16),
        ),
        got,
        dy,
        state,
        flops=50_000_000,
        touched=500_000,
    )
    back = exchange(reply, "tx").reshape(slots, -1)
    h1, h2 = call(
        hidden_kernel,
        (shape((slots, w_in.shape[1]), BF16),) * 2,
        profile,
        w_in,
        b_in,
        w_mid,
        b_mid,
        w_out,
        flops=130_000_000,
        touched=1_000_000,
    )
    terms = lax.all_gather(terms[:cap], "ty").sum(axis=0)
    other = lax.ppermute(terms, "tx", [(a, a ^ 1) for a in range(peers)])
    is_even = lax.axis_index("tx") % 2 == 0
    even = jnp.where(is_even, terms, other)
    odd = jnp.where(is_even, other, terms)
    state_grad, radiance, bias_grad = call(
        functools.partial(final_kernel, scale),
        (
            shape((columns, feat), F32),
            shape((slots, channels), BF16),
            shape((npred, channels), F32),
        ),
        back,
        got,
        h1,
        h2,
        even,
        odd,
        w_in,
        b_in,
        w_mid,
        b_mid,
        w_out,
        b_out,
        flops=400_000_000,
        touched=2_000_000,
    )
    return (radiance, state_grad, bias_grad)


def solution(mesh):
    both = P(("tx", "ty"), None)
    placed = (both, both, both, both, P(("tx", "ty")), P(None, ("tx", "ty"))) + (P(),) * 6
    return jax.shard_map(
        on_device,
        mesh=mesh,
        in_specs=placed,
        out_specs=(both, both, P()),
        check_vma=False,
    )
```

```python
import functools
import math

import jax
import jax.numpy as jnp
from jax import lax
from jax.experimental import pallas as pl
from jax.experimental.pallas import tpu as pltpu
from jax.sharding import PartitionSpec as P

F32, BF16, I32 = jnp.float32, jnp.bfloat16, jnp.int32
NT = (((1,), (1,)), ((), ()))
TN = (((0,), (0,)), ((), ()))
TILE_W = 32
LANES = 128
GRANT = 40 * 1024 * 1024
PACK_GRANT = 60 * 1024 * 1024


def exchange(block, axis):
    return lax.all_to_all(block, axis, split_axis=0, concat_axis=0, tiled=True)


def dot(a, b):
    return jnp.dot(a, b, preferred_element_type=F32)


def dot_dims(a, b, dims):
    return lax.dot_general(a, b, dims, preferred_element_type=F32)


def place(shape, dim):
    return lax.broadcasted_iota(I32, shape, dim)


def identity(rows, columns):
    shape = (rows, columns)
    return (place(shape, 0) == place(shape, 1)).astype(F32).astype(BF16)


def rounded(x):
    return x.astype(BF16).astype(F32)


def masked_by(departures, counts):
    slots, peers = departures.shape[0], counts.shape[1]
    cap = slots // peers
    holds = (place((slots, peers), 0) // cap == place((slots, peers), 1)).astype(F32).astype(BF16)
    counted = jnp.broadcast_to(counts[...].astype(F32), (8, peers)).astype(BF16)
    count_of = dot_dims(holds, counted, NT)[:, 0:1]
    live = (place((slots, 1), 0) % cap).astype(F32) < count_of
    return jnp.where(live, departures[...].astype(F32), 0.0).astype(BF16)


def keep_kernel(state, departures, counts, b_in, b_mid, b_out, state_kept, dy, in_kept, mid_kept, out_kept):
    state_kept[...] = state[...]
    in_kept[...] = b_in[...]
    mid_kept[...] = b_mid[...]
    out_kept[...] = b_out[...]
    dy[...] = masked_by(departures, counts)


def pack_kernel(
    departures_hbm, stencil_hbm, bilinear_hbm, counts_hbm, predictors_hbm, out,
    departures, stencil, bilinear, counts, predictors, arrived
):
    pairs = (
        (counts_hbm, counts),
        (departures_hbm, departures),
        (predictors_hbm, predictors),
        (stencil_hbm, stencil),
        (bilinear_hbm, bilinear),
    )
    copies = [
        pltpu.make_async_copy(source, target, arrived.at[k])
        for k, (source, target) in enumerate(pairs)
    ]
    for copy in copies:
        copy.start()
    slots, channels = departures.shape
    peers = counts.shape[1]
    cap = slots // peers
    npred = predictors.shape[0]
    turn = identity(slots, slots)
    for copy in copies:
        copy.wait()
    dy = masked_by(departures, counts)

    pred = predictors[...]
    part0 = rounded(pred)
    part1 = rounded(pred - part0)
    part2 = pred - part0 - part1
    thirds = dot(jnp.concatenate([part0, part1, part2], axis=0).astype(BF16), dy)
    partial = thirds[:npred] + thirds[npred : 2 * npred] + thirds[2 * npred :]
    slot = place((slots, npred), 0) % (2 * cap) * 2
    which = place((slots, npred), 1)
    partial = partial.astype(BF16)
    for k in range(2):
        chosen = (which == slot + k).astype(F32).astype(BF16)
        out[:, :, LANES + k * channels : LANES + (k + 1) * channels] = (
            dot(chosen, partial).astype(BF16).reshape(peers, cap, channels)
        )

    corner = stencil[0:1, :]
    column = jnp.bitwise_and(corner, TILE_W - 1)
    row = (corner - column) // TILE_W
    rows = [bilinear[...].astype(F32), row.astype(F32), column.astype(F32)]
    rows.append(jnp.zeros((LANES - 6, slots), F32))
    extra = jnp.concatenate(rows, axis=0).astype(BF16)
    out[:, :, :LANES] = dot_dims(turn, extra, NT).astype(BF16).reshape(peers, cap, LANES)


def spread_of(extra, columns):
    extra = extra.astype(F32)
    corner = (extra[:, 4:5] * TILE_W + extra[:, 5:6]).astype(I32)
    delta = place((extra.shape[0], columns), 1) - corner
    spread = jnp.zeros(delta.shape, F32)
    for k, offset in enumerate((0, 1, TILE_W, TILE_W + 1)):
        spread = jnp.where(delta == offset, extra[:, k : k + 1], spread)
    return spread.astype(BF16)


def reply_kernel(cap, got, dy, state, out, terms, kept):
    slots = got.shape[0]
    feat = state.shape[1]
    mine = (place((8, slots), 1) % cap == place((8, slots), 0)).astype(F32).astype(BF16)
    terms[...] = dot(mine, got[:, LANES:])
    spread = spread_of(got[:, :LANES], state.shape[0])
    shape = out.shape[:2]
    profile = dot(spread, state[...]).astype(BF16)
    kept[...] = profile
    out[:, :, :feat] = profile.reshape(*shape, feat)
    out[:, :, feat:] = dy[...].reshape(*shape, dy.shape[1])


def forward(profile, w_in, b_in, w_mid, b_mid):
    h1 = jnp.tanh(dot(profile, w_in[...]) + b_in[...]).astype(BF16)
    h2 = jnp.tanh(dot(h1, w_mid[...]) + b_mid[...]).astype(BF16)
    return h1, h2


def hidden_kernel(profile, w_in, b_in, w_mid, b_mid, w_out, h1, h2):
    del w_out
    h1[...], h2[...] = forward(profile[...], w_in, b_in, w_mid, b_mid)


def final_kernel(
    back, got, h1, h2, w_in, b_in, w_mid, b_mid, w_out, b_out, state_grad, radiance, one
):
    feat = w_in.shape[0]
    h2f, h1f = h2[...].astype(F32), h1[...].astype(F32)
    g2 = dot_dims(back[:, feat:], w_out[...], NT)
    g2 = (g2 * (1.0 - h2f * h2f)).astype(BF16)
    g1 = dot_dims(g2, w_mid[...], NT)
    g1 = (g1 * (1.0 - h1f * h1f)).astype(BF16)
    dprofile = dot_dims(g1, w_in[...], NT).astype(BF16)
    spread = spread_of(got[:, :LANES], state_grad.shape[0])
    state_grad[...] = dot_dims(spread, dprofile, TN)

    _, last = forward(back[:, :feat], w_in, b_in, w_mid, b_mid)
    radiance[...] = (dot(last, w_out[...]) + b_out[...]).astype(BF16)
    one[...] = jnp.ones(one.shape, F32)


def bias_kernel(scale, one, even, odd, bias_grad):
    channels = bias_grad.shape[1]
    scale = one[0:1, 0:1] * scale
    for k, half in enumerate((even, odd)):
        for j in range(2):
            for e in range(2):
                row = 4 * k + 2 * j + e
                bias_grad[row : row + 1, :] = (
                    half[j : j + 1, e * channels : (e + 1) * channels] * scale
                )


def call(kernel, out, *args, flops=0, touched=0, space=pltpu.VMEM, scratch=(), grant=GRANT):
    return pl.pallas_call(
        kernel,
        out_shape=out,
        in_specs=[pl.BlockSpec(memory_space=space)] * len(args),
        out_specs=jax.tree.map(lambda _: pl.BlockSpec(memory_space=pltpu.VMEM), out),
        scratch_shapes=scratch,
        compiler_params=pltpu.CompilerParams(vmem_limit_bytes=grant),
        cost_estimate=pl.CostEstimate(flops=flops, bytes_accessed=touched, transcendentals=0),
    )(*args)


def on_device(
    state, departures, stencil, bilinear, counts, predictors, w_in, b_in, w_mid, b_mid, w_out, b_out
):
    slots, channels = departures.shape
    columns, feat = state.shape
    npred = predictors.shape[0]
    peers, rows = lax.axis_size("tx"), lax.axis_size("ty")
    cap = slots // peers
    scale = 1.0 / math.sqrt(slots * peers * rows)
    b_in, b_mid, b_out = b_in[None], b_mid[None], b_out[None]
    shape = jax.ShapeDtypeStruct

    inputs = (departures, stencil.T, bilinear.T, counts[None], predictors)
    packed = call(
        pack_kernel,
        shape((peers, cap, LANES + 2 * channels), BF16),
        *inputs,
        flops=40_000_000,
        touched=300_000,
        space=pl.ANY,
        scratch=[pltpu.VMEM(a.shape, a.dtype) for a in inputs]
        + [pltpu.SemaphoreType.DMA((len(inputs),))],
        grant=PACK_GRANT,
    )
    state, dy, b_in, b_mid, b_out = call(
        keep_kernel,
        (shape(state.shape, BF16), shape(departures.shape, BF16))
        + tuple(shape(b.shape, F32) for b in (b_in, b_mid, b_out)),
        state,
        departures,
        counts[None],
        b_in,
        b_mid,
        b_out,
        flops=2_000_000_000,
        touched=2_000_000,
    )
    got = exchange(packed, "tx").reshape(slots, -1)
    reply, terms, profile = call(
        functools.partial(reply_kernel, cap),
        (
            shape((peers, cap, feat + channels), BF16),
            shape((8, 2 * channels), F32),
            shape((slots, feat), BF16),
        ),
        got,
        dy,
        state,
        flops=50_000_000,
        touched=500_000,
    )
    back = exchange(reply, "tx").reshape(slots, -1)
    h1, h2 = call(
        hidden_kernel,
        (shape((slots, w_in.shape[1]), BF16),) * 2,
        profile,
        w_in,
        b_in,
        w_mid,
        b_mid,
        w_out,
        flops=130_000_000,
        touched=1_000_000,
    )
    terms = lax.all_gather(terms[:cap], "ty").sum(axis=0)
    terms, back = lax.optimization_barrier((terms, back))
    other = lax.ppermute(terms, "tx", [(a, a ^ 1) for a in range(peers)])
    is_even = lax.axis_index("tx") % 2 == 0
    even = jnp.where(is_even, terms, other)
    odd = jnp.where(is_even, other, terms)
    state_grad, radiance, one = call(
        final_kernel,
        (shape((columns, feat), F32), shape((slots, channels), BF16), shape((8, LANES), F32)),
        back,
        got,
        h1,
        h2,
        w_in,
        b_in,
        w_mid,
        b_mid,
        w_out,
        b_out,
        flops=3_000_000_000,
        touched=2_000_000,
    )
    bias_grad = call(
        functools.partial(bias_kernel, scale),
        shape((npred, channels), F32),
        one,
        even,
        odd,
        flops=2_000,
        touched=20_000,
    )
    return (radiance, state_grad, bias_grad)


def solution(mesh):
    both = P(("tx", "ty"), None)
    placed = (both, both, both, both, P(("tx", "ty")), P(None, ("tx", "ty"))) + (P(),) * 6
    return jax.shard_map(
        on_device,
        mesh=mesh,
        in_specs=placed,
        out_specs=(both, both, P()),
        check_vma=False,
    )
```
